512 devices in a mesh: dp: 32 (over x, z), etp: 16 (over y, core).
Axes of the slice: x: 4, y: 8, z: 8, core: 2. Of those that a mesh axis runs over, the one named last changes fastest.
Arguments:
- momentum: float32 [32, 3584, 1536], P('dp', 'etp'), may hold values from -6 to 6
- grad: bfloat16 [32, 3584, 1536], P('dp', 'etp'), may hold values from -3100 to 3100
- q_in: float32 [32, 1536, 64], P('dp'), may hold values from -0.15625 to 0.15625
Outputs:
- momentum_out: float32 [32, 3584, 1536], P('dp', 'etp')
- q_out: float32 [32, 1536, 64], P('dp')
- update: bfloat16 [32, 3584, 1536], P('dp', 'etp')
The draws below stay inside these ranges and needn't reach their ends.
All inputs are finite; a program needn't handle non-finite values.
Results may differ from the reference program's by a relative error of at most 0.0045.
Values sent between devices are 32-bit elements; how exact they have to be, the bound alone decides.
A program may use at most 64 MiB of HBM per device.

```python
import math
import jax
import jax.numpy as jnp
from jax import lax

ROWS = 3584
COLS = 1536
RANK = 64
ITERS = 8
EXPERTS = 32


def draw_grad(key, part):
    key = jax.random.fold_in(key, 7)
    keys = jax.random.split(key, 3)
    shape = (EXPERTS, ROWS, COLS)
    row_frac = jnp.arange(ROWS, dtype=jnp.float32)[None, :, None] / ROWS
    expert_frac = jnp.arange(EXPERTS, dtype=jnp.float32)[:, None, None] / max(EXPERTS - 1, 1)
    row_scale = 10.0 ** (0.5 * row_frac + 0.5 * jax.random.uniform(keys[1], (EXPERTS, ROWS, 1), jnp.float32))
    col_scale = 10.0 ** jax.random.uniform(keys[2], (EXPERTS, 1, COLS), jnp.float32)
    values = jax.random.truncated_normal(keys[0], -5.0, 5.0, shape, jnp.float32)
    return (values * row_scale * col_scale * 3.0 ** expert_frac).astype(jnp.bfloat16)


def levels(rng, shape, cuts, low, high):
    gain, own = 1.0, jax.random.fold_in(rng, 6)
    for position, shards_of in cuts:
        draws = jnp.exp(jax.random.uniform(jax.random.fold_in(own, position), (shards_of,), jnp.float32, low / len(cuts), high / len(cuts)))
        gain = gain * jnp.repeat(draws, shape[position] // shards_of).reshape([-1 if axis == position else 1 for axis in range(len(shape))])
    return gain


def centred(own_key, shape, scale, limit, shards=(), held_as=jnp.bfloat16):
    factor_of = levels(own_key, shape, shards, -0.22, 0.18) if shards else 1.0
    values = jax.random.normal(own_key, shape, jnp.float32) * scale * factor_of
    return jnp.minimum(jnp.maximum(values, -limit), limit).astype(held_as)


def setup_inputs(seed: int = 0) -> dict:
    seeds = jax.random.split(jax.random.key(seed), 4)
    momentum = centred(seeds[0], (EXPERTS, ROWS, COLS), 1.0, 6.0, ((0, 32), (1, 16)), jnp.float32)
    grad = draw_grad(jax.random.fold_in(seeds[3], 71), 0)
    q_in = centred(seeds[2], (EXPERTS, COLS, RANK), COLS ** -0.5, 0.15625, ((0, 32),), jnp.float32)
    return dict(momentum=momentum, grad=grad, q_in=q_in)


keep_rate = 0.9
epsilon = 1e-06

def matmul(former, latter):
    return jnp.dot(former.astype(jnp.float32), latter.astype(jnp.float32), precision=lax.Precision.HIGHEST, preferred_element_type=jnp.float32)

def reference(momentum, grad, q_in):
    element_count = float(EXPERTS * ROWS * COLS)
    square_sums = lax.map(lambda block: jnp.sum(jnp.square(block.astype(jnp.float32))), grad)
    total_sq = jnp.sum(square_sums)
    clip_factor = jnp.minimum(1.0, lax.rsqrt(total_sq / element_count + epsilon))

    def one_expert(items):
        momentum_one, grad_one, right_basis = items
        blended = momentum_one + clip_factor * grad_one.astype(jnp.float32)
        left_basis = None
        across = None
        for turn_index in range(ITERS):
            raw_left = matmul(blended, right_basis)
            gram_matrix = matmul(raw_left.T, raw_left)
            lower_factor = jnp.linalg.cholesky(gram_matrix)
            left_basis = lax.linalg.triangular_solve(lower_factor, raw_left, left_side=False, lower=True, transpose_a=True)
            across = matmul(blended.T, left_basis)
            column_sq = lax.optimization_barrier(jnp.sum(across * across, axis=0))
            right_basis = across * lax.rsqrt(column_sq + epsilon)[None, :]
        momentum_new = blended - (1.0 - keep_rate) * matmul(left_basis, across.T)
        update_new = (math.sqrt(ROWS * COLS / RANK) * matmul(left_basis, right_basis.T)).astype(jnp.bfloat16)
        return (momentum_new, right_basis, update_new)
    results = lax.map(one_expert, (momentum, grad, q_in))
    return (results[0], results[1], results[2])
```

```python
import functools
import math

import jax
import jax.numpy as jnp
from jax import lax
from jax.experimental import pallas as pl
from jax.experimental.pallas import tpu as pltpu
from jax.sharding import PartitionSpec as P

ROWS = 3584
COLS = 1536
RANK = 64
ITERS = 8
DIRECT = 3

BLOCK = 128
BLOCKS = COLS // BLOCK
TILES = 5
RING = 8

keep_rate = 0.9
epsilon = 1e-06

MESH = pl.DeviceIdType.MESH
HIGHEST = lax.Precision.HIGHEST
F32 = jnp.float32
BF16 = jnp.bfloat16


def nn(former, latter, precision=None):
    return jnp.dot(former, latter, precision=precision, preferred_element_type=F32)


def nt(former, latter, precision=None):
    return lax.dot_general(
        former, latter, (((1,), (1,)), ((), ())), precision=precision, preferred_element_type=F32
    )


def split(values):
    high = values.astype(BF16)
    rest = values - high.astype(F32)
    middle = rest.astype(BF16)
    low = (rest - middle.astype(F32)).astype(BF16)
    return high, middle, low


def inverse_cholesky(gram):
    full = (8, 2 * RANK)
    ones = lax.broadcasted_iota(jnp.int32, (RANK, RANK), 0) == lax.broadcasted_iota(
        jnp.int32, (RANK, RANK), 1
    )
    joined = jnp.concatenate([gram, ones.astype(F32)], axis=1)
    panels = [joined[8 * p : 8 * p + 8] for p in range(RANK // 8)]
    sublane = lax.broadcasted_iota(jnp.int32, full, 0)
    for p in range(RANK // 8):
        panel = panels[p]
        entry = [[None] * 8 for _ in range(8)]
        for i in range(8):
            for j in range(i + 1):
                entry[i][j] = jnp.broadcast_to(panel[i : i + 1, 8 * p + j : 8 * p + j + 1], full)
        rows = [jnp.broadcast_to(panel[i : i + 1, :], full) for i in range(8)]
        scale = [None] * 8
        factor = [[None] * 8 for _ in range(8)]
        for j in range(8):
            scale[j] = lax.rsqrt(entry[j][j])
            for i in range(j + 1, 8):
                factor[i][j] = entry[i][j] * scale[j]
            for i in range(j + 1, 8):
                for m in range(j + 1, i + 1):
                    entry[i][m] = entry[i][m] - factor[i][j] * factor[m][j]
            rows[j] = rows[j] * scale[j]
            for i in range(j + 1, 8):
                rows[i] = rows[i] - factor[i][j] * rows[j]
        done = rows[0]
        for i in range(1, 8):
            done = jnp.where(sublane == i, rows[i], done)
        panels[p] = done
        for q in range(p + 1, RANK // 8):
            column = [
                jnp.broadcast_to(panels[q][:, 8 * p + j : 8 * p + j + 1], full) for j in range(8)
            ]
            for j in range(8):
                column[j] = column[j] * scale[j]
                for i in range(j + 1, 8):
                    column[i] = column[i] - factor[i][j] * column[j]
            left = panels[q]
            for j in range(8):
                left = left - column[j] * rows[j]
            panels[q] = left
    return jnp.concatenate(panels, axis=0)[:, RANK:]


def refresh_kernel(
    dp_size,
    element_count,
    m_ref,
    g_ref,
    q_ref,
    s_out,
    a_out,
    r_out,
    clip_out,
    wide,
    other_m,
    other_g,
    sums,
    totals,
    tall,
    flat,
    mine,
    ring_in,
    ring_out,
    tiles,
    sib_tiles,
    w_high,
    w_mid,
    w_low,
    r_ref,
    z_ref,
    v_ref,
    a_ref,
    small_send,
    small_recv,
    big_send,
    big_recv,
    ring_send,
    ring_recv,
    gather_send,
    gather_recv,
    sib_send,
    sib_recv,
):
    me = lax.axis_index("etp")
    dp = lax.axis_index("dp")
    etp_size = 2 * RING
    chip = me // 2
    core = lax.rem(me, 2)
    sibling = chip * 2 + (1 - core)
    way = 1 - 2 * core
    ahead = lax.rem(chip + way + RING, RING) * 2 + core
    rows = m_ref.shape[0]

    barrier = pltpu.get_barrier_semaphore()

    @pl.loop(1, etp_size)
    def _(step):
        pl.semaphore_signal(
            barrier, inc=1, device_id={"etp": lax.rem(me + step, etp_size)}, device_id_type=MESH
        )

    @pl.loop(1, dp_size)
    def _(step):
        pl.semaphore_signal(
            barrier, inc=1, device_id={"dp": lax.rem(dp + step, dp_size)}, device_id_type=MESH
        )

    wide[...] = g_ref[...].astype(F32)
    partial = jnp.zeros((8, BLOCK), F32)
    for b in range(BLOCKS):
        piece = wide[:, BLOCK * b : BLOCK * (b + 1)]
        partial = partial + jnp.sum((piece * piece).reshape(rows // 8, 8, BLOCK), axis=0)
    sums[me] = partial

    pl.semaphore_wait(barrier, etp_size + dp_size - 2)

    @pl.loop(1, etp_size)
    def _(step):
        pltpu.make_async_remote_copy(
            src_ref=sums.at[me],
            dst_ref=sums.at[me],
            send_sem=small_send.at[0],
            recv_sem=small_recv.at[0],
            device_id={"etp": lax.rem(me + step, etp_size)},
            device_id_type=MESH,
        ).start()

    copies = [
        pltpu.make_async_remote_copy(
            src_ref=source,
            dst_ref=target,
            send_sem=big_send.at[n],
            recv_sem=big_recv.at[n],
            device_id={"etp": sibling},
            device_id_type=MESH,
        )
        for n, (source, target) in enumerate(((m_ref, other_m), (wide, other_g)))
    ]
    for copy in copies:
        copy.start()

    others = sums.at[pl.ds(0, etp_size - 1)]
    pltpu.make_async_copy(others, others, small_recv.at[0]).wait()
    group = sums[0]
    for n in range(1, etp_size):
        group = group + sums[n]
    totals[dp] = group

    if dp_size > 1:

        @pl.loop(1, dp_size)
        def _(step):
            pltpu.make_async_remote_copy(
                src_ref=totals.at[dp],
                dst_ref=totals.at[dp],
                send_sem=small_send.at[1],
                recv_sem=small_recv.at[1],
                device_id={"dp": lax.rem(dp + step, dp_size)},
                device_id_type=MESH,
            ).start()

        far = totals.at[pl.ds(0, dp_size - 1)]
        pltpu.make_async_copy(far, far, small_recv.at[1]).wait()
        pltpu.make_async_copy(far, far, small_send.at[1]).wait()
    pltpu.make_async_copy(others, others, small_send.at[0]).wait()
    everything = totals[0]
    for n in range(1, dp_size):
        everything = everything + totals[n]
    total_sq = jnp.sum(jnp.sum(everything, axis=0, keepdims=True), axis=1, keepdims=True)
    clip = jnp.minimum(1.0, lax.rsqrt(total_sq / element_count + epsilon))
    clip_out[...] = jnp.broadcast_to(clip, (8, BLOCK))
    for copy in copies:
        copy.wait()

    for b in range(BLOCKS):
        columns = slice(BLOCK * b, BLOCK * (b + 1))
        own = m_ref[:, columns] + clip * wide[:, columns]
        sib = other_m[:, columns] + clip * other_g[:, columns]
        blended = jnp.concatenate([own, sib], axis=0)
        for n, part in enumerate(split(blended)):
            tall[b, :, BLOCK * n : BLOCK * (n + 1)] = part
        for n, part in enumerate(split(blended.T)):
            flat[b, BLOCK * n : BLOCK * (n + 1), :] = part

    def place(chunk, of_core, s):
        tile = TILES * (2 * chunk + of_core) + s
        row = lax.rem(tile, BLOCKS)
        return row, lax.rem(row + tile // BLOCKS, BLOCKS)

    def own_tiles(chunk):
        for s in range(TILES):
            row, column = place(chunk, core, s)
            both = nn(flat[row], tall[column])
            part = lambda i, j: both[BLOCK * i : BLOCK * (i + 1), BLOCK * j : BLOCK * (j + 1)]
            mine[s] = (
                part(0, 0) + ((part(0, 1) + part(1, 0)) + (part(1, 1) + (part(0, 2) + part(2, 0))))
            )

    def ring_copy(step, s):
        return pltpu.make_async_remote_copy(
            src_ref=ring_out.at[step, s],
            dst_ref=ring_in.at[step, s],
            send_sem=ring_send,
            recv_sem=ring_recv.at[step, s],
            device_id={"etp": ahead},
            device_id_type=MESH,
        )

    own_tiles(lax.rem(chip - way + RING, RING))
    for s in range(TILES):
        ring_out[0, s] = mine[s]
        ring_copy(0, s).start()

    @pl.loop(1, RING - 1)
    def _(step):
        own_tiles(lax.rem(chip - way * (1 + step) + 2 * RING, RING))
        for s in range(TILES):
            ring_copy(step - 1, s).wait_recv()
            ring_out[step, s] = mine[s] + ring_in[step - 1, s]
            ring_copy(step, s).start()

    def gather_copy(step, s):
        chunk = lax.rem(chip - way * step + 2 * RING, RING)
        return pltpu.make_async_remote_copy(
            src_ref=tiles.at[chunk, s],
            dst_ref=tiles.at[chunk, s],
            send_sem=gather_send,
            recv_sem=gather_recv.at[step, s],
            device_id={"etp": ahead},
            device_id_type=MESH,
        )

    def arrival(step, s):
        chunk = lax.rem(chip - way * (step + 1) + 2 * RING, RING)
        return pltpu.make_async_remote_copy(
            src_ref=tiles.at[chunk, s],
            dst_ref=tiles.at[chunk, s],
            send_sem=gather_send,
            recv_sem=gather_recv.at[step, s],
            device_id={"etp": ahead},
            device_id_type=MESH,
        )

    def sib_copy(step, s):
        chunk = lax.rem(chip - way * step + 2 * RING, RING)
        return pltpu.make_async_remote_copy(
            src_ref=tiles.at[chunk, s],
            dst_ref=sib_tiles.at[chunk, s],
            send_sem=sib_send,
            recv_sem=sib_recv.at[step, s],
            device_id={"etp": sibling},
            device_id_type=MESH,
        )

    def sib_arrival(step, s):
        chunk = lax.rem(chip + way * step + 2 * RING, RING)
        return pltpu.make_async_remote_copy(
            src_ref=tiles.at[chunk, s],
            dst_ref=sib_tiles.at[chunk, s],
            send_sem=sib_send,
            recv_sem=sib_recv.at[step, s],
            device_id={"etp": sibling},
            device_id_type=MESH,
        )

    def expand(store, chunk, of_core, s):
        row, column = place(chunk, of_core, s)
        tile = store[chunk, s]
        for target, part in zip((w_high, w_mid, w_low), split(tile)):
            target[row, column] = part
        for target, part in zip((w_high, w_mid, w_low), split(tile.T)):
            target[column, row] = part

    own_tiles(chip)
    for s in range(TILES):
        ring_copy(RING - 2, s).wait_recv()
        tiles[chip, s] = mine[s] + ring_in[RING - 2, s]
        gather_copy(0, s).start()
        sib_copy(0, s).start()

    @pl.loop(0, RING)
    def _(step):
        chunk = lax.rem(chip - way * step + 2 * RING, RING)
        sib_chunk = lax.rem(chip + way * step + 2 * RING, RING)
        for s in range(TILES):
            expand(tiles, chunk, core, s)
        for s in range(TILES):
            sib_arrival(step, s).wait_recv()
            expand(sib_tiles, sib_chunk, 1 - core, s)

        @pl.when(step < RING - 1)
        def _():
            for s in range(TILES):
                arrival(step, s).wait_recv()
                sib_copy(step + 1, s).start()

        @pl.when(step < RING - 2)
        def _():
            for s in range(TILES):
                gather_copy(step + 1, s).start()

    def through_gram(values, target):
        high, middle, low = split(values)
        three = jnp.concatenate([high, middle, low], axis=0)
        two = jnp.concatenate([high, middle], axis=0)
        for n in range(BLOCKS // 2):
            def wide_block(store):
                return jnp.concatenate(
                    [
                        jnp.concatenate([store[i, 2 * n], store[i, 2 * n + 1]], axis=1)
                        for i in range(BLOCKS)
                    ],
                    axis=0,
                )
            first = nn(three, wide_block(w_high))
            second = nn(two, wide_block(w_mid))
            third = nn(high, wide_block(w_low))
            result = first[:RANK] + (
                (first[RANK : 2 * RANK] + second[:RANK])
                + ((first[2 * RANK :] + second[RANK:]) + third)
            )
            target[:, 2 * BLOCK * n : 2 * BLOCK * (n + 1)] = result

    def gram_of(former, latter):
        both = nt(
            jnp.concatenate(split(former), axis=0), jnp.concatenate(split(latter), axis=0)
        )
        part = lambda i, j: both[RANK * i : RANK * (i + 1), RANK * j : RANK * (j + 1)]
        return part(0, 0) + (
            (part(0, 1) + part(1, 0)) + (part(1, 1) + (part(0, 2) + part(2, 0)))
        )

    r_ref[...] = q_ref[...].T

    def normalise(inverse):
        a_ref[...] = nn(inverse, z_ref[...], HIGHEST)
        across = a_ref[...]
        norm = jnp.sum(across * across, axis=1, keepdims=True) + epsilon
        return across, lax.rsqrt(norm)

    @pl.loop(0, DIRECT)
    def _(turn):
        through_gram(r_ref[...], z_ref)
        inverse = inverse_cholesky(gram_of(r_ref[...], z_ref[...]))
        across, scale = normalise(inverse)
        r_ref[...] = across * scale

    through_gram(r_ref[...], z_ref)

    @pl.loop(DIRECT, ITERS - 1)
    def _(turn):
        through_gram(z_ref[...], v_ref)
        inverse = inverse_cholesky(gram_of(r_ref[...], z_ref[...]))
        across, scale = normalise(inverse)
        r_ref[...] = across * scale
        z_ref[...] = nn(inverse * scale, v_ref[...], HIGHEST)

    inverse = inverse_cholesky(gram_of(r_ref[...], z_ref[...]))
    s_out[...] = nn(inverse, r_ref[...], HIGHEST)
    across, scale = normalise(inverse)
    a_out[...] = across
    r_out[...] = across * scale

    for copies_of, store in ((ring_send, ring_out), (gather_send, tiles)):
        sent = store.at[pl.ds(0, RING - 1)]
        pltpu.make_async_copy(sent, sent, copies_of).wait()
    pltpu.make_async_copy(tiles, tiles, sib_send).wait()


def finish_kernel(m_ref, g_ref, clip_ref, s_ref, a_ref, r_ref, m_out, q_out, u_out):
    clip = clip_ref[0:1, 0:1]
    blended = m_ref[...] + clip * g_ref[...].astype(F32)
    left = nt(blended, s_ref[...], HIGHEST)
    m_out[...] = blended - (1.0 - keep_rate) * nn(left, a_ref[...], HIGHEST)
    update_scale = math.sqrt(ROWS * COLS / RANK)
    u_out[...] = (update_scale * nn(left, r_ref[...], HIGHEST)).astype(BF16)
    q_out[...] = r_ref[...].T


def body(momentum, grad, q_in):
    dp_size = lax.axis_size("dp")
    rows, cols = momentum.shape[1:]
    element_count = float(dp_size * rows * 2 * RING * cols)
    m, g, q = momentum[0], grad[0], q_in[0]
    vmem = pl.BlockSpec(memory_space=pltpu.VMEM)
    tile = (BLOCK, BLOCK)
    s_t, a_t, r_t, clip = pl.pallas_call(
        functools.partial(refresh_kernel, dp_size, element_count),
        out_shape=[jax.ShapeDtypeStruct((RANK, cols), F32)] * 3
        + [jax.ShapeDtypeStruct((8, BLOCK), F32)],
        in_specs=[vmem] * 3,
        out_specs=[vmem] * 4,
        scratch_shapes=[
            pltpu.VMEM((rows, cols), F32),
            pltpu.VMEM((rows, cols), F32),
            pltpu.VMEM((rows, cols), F32),
            pltpu.VMEM((2 * RING, 8, BLOCK), F32),
            pltpu.VMEM((dp_size, 8, BLOCK), F32),
            pltpu.VMEM((BLOCKS, 2 * rows, 3 * BLOCK), BF16),
            pltpu.VMEM((BLOCKS, 3 * BLOCK, 2 * rows), BF16),
            pltpu.VMEM((TILES,) + tile, F32),
            pltpu.VMEM((RING - 1, TILES) + tile, F32),
            pltpu.VMEM((RING - 1, TILES) + tile, F32),
            pltpu.VMEM((RING, TILES) + tile, F32),
            pltpu.VMEM((RING, TILES) + tile, F32),
            pltpu.VMEM((BLOCKS, BLOCKS) + tile, BF16),
            pltpu.VMEM((BLOCKS, BLOCKS) + tile, BF16),
            pltpu.VMEM((BLOCKS, BLOCKS) + tile, BF16),
            pltpu.VMEM((RANK, cols), F32),
            pltpu.VMEM((RANK, cols), F32),
            pltpu.VMEM((RANK, cols), F32),
            pltpu.VMEM((RANK, cols), F32),
            pltpu.SemaphoreType.DMA((2,)),
            pltpu.SemaphoreType.DMA((2,)),
            pltpu.SemaphoreType.DMA((2,)),
            pltpu.SemaphoreType.DMA((2,)),
            pltpu.SemaphoreType.DMA,
            pltpu.SemaphoreType.DMA((RING - 1, TILES)),
            pltpu.SemaphoreType.DMA,
            pltpu.SemaphoreType.DMA((RING - 1, TILES)),
            pltpu.SemaphoreType.DMA,
            pltpu.SemaphoreType.DMA((RING, TILES)),
        ],
        compiler_params=pltpu.CompilerParams(
            collective_id=0, has_side_effects=True, vmem_limit_bytes=58 << 20
        ),
    )(m, g, q)
    part = rows // 2
    whole = lambda shape: pl.BlockSpec(shape, lambda n: (0, 0))
    by_rows = pl.BlockSpec((part, cols), lambda n: (n, 0))
    m_new, q_new, update = pl.pallas_call(
        finish_kernel,
        grid=(2,),
        out_shape=[
            jax.ShapeDtypeStruct((rows, cols), F32),
            jax.ShapeDtypeStruct((cols, RANK), F32),
            jax.ShapeDtypeStruct((rows, cols), BF16),
        ],
        in_specs=[by_rows, by_rows, whole((8, BLOCK))] + [whole((RANK, cols))] * 3,
        out_specs=[by_rows, whole((cols, RANK)), by_rows],
        compiler_params=pltpu.CompilerParams(vmem_limit_bytes=58 << 20),
    )(m, g, clip, s_t, a_t, r_t)
    return m_new[None], q_new[None], update[None]


def solution(mesh):
    return jax.shard_map(
        body,
        mesh=mesh,
        in_specs=(P("dp", "etp", None), P("dp", "etp", None), P("dp", None, None)),
        out_specs=(P("dp", "etp", None), P("dp", None, None), P("dp", "etp", None)),
        check_vma=False,
    )
```

```python
import functools
import math

import jax
import jax.numpy as jnp
from jax import lax
from jax.experimental import pallas as pl
from jax.experimental.pallas import tpu as pltpu
from jax.sharding import PartitionSpec as P

ROWS = 3584
COLS = 1536
RANK = 64
ITERS = 8
DIRECT = 3

BLOCK = 128
BLOCKS = COLS // BLOCK
TILES = 5
HALVES = 2
RING = 8
LONG = RING // 2
SHORT = RING - 1 - LONG

keep_rate = 0.9
epsilon = 1e-06

MESH = pl.DeviceIdType.MESH
F32 = jnp.float32
BF16 = jnp.bfloat16


def nn(former, latter):
    return jnp.dot(former, latter, preferred_element_type=F32)


def nt(former, latter):
    return lax.dot_general(former, latter, (((1,), (1,)), ((), ())), preferred_element_type=F32)


def split(values, terms):
    parts = []
    for _ in range(terms):
        parts.append(values.astype(BF16))
        values = values - parts[-1].astype(F32)
    return parts


def inverse_cholesky(gram, between=()):
    full = (8, 2 * RANK)
    ones = lax.broadcasted_iota(jnp.int32, (RANK, RANK), 0) == lax.broadcasted_iota(
        jnp.int32, (RANK, RANK), 1
    )
    joined = jnp.concatenate([gram, ones.astype(F32)], axis=1)
    panels = [joined[8 * p : 8 * p + 8] for p in range(RANK // 8)]
    sublane = lax.broadcasted_iota(jnp.int32, full, 0)
    for p in range(RANK // 8):
        if p < len(between):
            between[p]()
        panel = panels[p]
        entry = [[None] * 8 for _ in range(8)]
        for i in range(8):
            for j in range(i + 1):
                entry[i][j] = jnp.broadcast_to(panel[i : i + 1, 8 * p + j : 8 * p + j + 1], full)
        rows = [jnp.broadcast_to(panel[i : i + 1, :], full) for i in range(8)]
        scale = [None] * 8
        factor = [[None] * 8 for _ in range(8)]
        for j in range(8):
            scale[j] = lax.rsqrt(entry[j][j])
            for i in range(j + 1, 8):
                factor[i][j] = entry[i][j] * scale[j]
            for i in range(j + 1, 8):
                for m in range(j + 1, i + 1):
                    entry[i][m] = entry[i][m] - factor[i][j] * factor[m][j]
            rows[j] = rows[j] * scale[j]
            for i in range(j + 1, 8):
                rows[i] = rows[i] - factor[i][j] * rows[j]
        done = rows[0]
        for i in range(1, 8):
            done = jnp.where(sublane == i, rows[i], done)
        panels[p] = done
        for q in range(p + 1, RANK // 8):
            column = [
                jnp.broadcast_to(panels[q][:, 8 * p + j : 8 * p + j + 1], full) for j in range(8)
            ]
            for j in range(8):
                column[j] = column[j] * scale[j]
                for i in range(j + 1, 8):
                    column[i] = column[i] - factor[i][j] * column[j]
            left = panels[q]
            for j in range(8):
                left = left - column[j] * rows[j]
            panels[q] = left
    return jnp.concatenate(panels, axis=0)[:, RANK:]


def refresh_kernel(
    dp_size,
    element_count,
    m_hbm,
    g_hbm,
    q_hbm,
    left_out,
    r_out,
    clip_out,
    m_ref,
    g_ref,
    q_ref,
    wide,
    other_m,
    other_g,
    sums,
    totals,
    tall,
    flat,
    own_far,
    own_near,
    far_in,
    far_out,
    near_in,
    near_out,
    tiles,
    sib_tiles,
    w_high,
    w_mid,
    r_terms,
    z_terms,
    v_terms,
    v_ref,
    load,
    small_send,
    small_recv,
    big_send,
    big_recv,
    ring_send,
    far_recv,
    near_recv,
    gather_send,
    gather_far_recv,
    gather_near_recv,
    sib_send,
    sib_recv,
):
    me = lax.axis_index("etp")
    dp = lax.axis_index("dp")
    etp_size = 2 * RING
    chip = me // 2
    core = lax.rem(me, 2)
    sibling = chip * 2 + (1 - core)
    way = 1 - 2 * core
    ahead = lax.rem(chip + way + RING, RING) * 2 + core
    behind = lax.rem(chip - way + RING, RING) * 2 + core
    rows = m_ref.shape[0]

    barrier = pltpu.get_barrier_semaphore()

    @pl.loop(1, etp_size)
    def _(step):
        pl.semaphore_signal(
            barrier, inc=1, device_id={"etp": lax.rem(me + step, etp_size)}, device_id_type=MESH
        )

    @pl.loop(1, dp_size)
    def _(step):
        pl.semaphore_signal(
            barrier, inc=1, device_id={"dp": lax.rem(dp + step, dp_size)}, device_id_type=MESH
        )

    loads = [
        pltpu.make_async_copy(source, target, load.at[n])
        for n, (source, target) in enumerate(((g_hbm, g_ref), (m_hbm, m_ref), (q_hbm, q_ref)))
    ]
    for copy in loads:
        copy.start()
    loads[0].wait()
    wide[...] = g_ref[...].astype(F32)
    partial = jnp.zeros((8, BLOCK), F32)
    for b in range(BLOCKS):
        piece = wide[:, BLOCK * b : BLOCK * (b + 1)]
        partial = partial + jnp.sum((piece * piece).reshape(rows // 8, 8, BLOCK), axis=0)
    sums[me] = partial
    loads[1].wait()
    loads[2].wait()

    pl.semaphore_wait(barrier, etp_size + dp_size - 2)

    @pl.loop(1, etp_size)
    def _(step):
        pltpu.make_async_remote_copy(
            src_ref=sums.at[me],
            dst_ref=sums.at[me],
            send_sem=small_send.at[0],
            recv_sem=small_recv.at[0],
            device_id={"etp": lax.rem(me + step, etp_size)},
            device_id_type=MESH,
        ).start()

    copies = [
        pltpu.make_async_remote_copy(
            src_ref=source,
            dst_ref=target,
            send_sem=big_send.at[n],
            recv_sem=big_recv.at[n],
            device_id={"etp": sibling},
            device_id_type=MESH,
        )
        for n, (source, target) in enumerate(((m_ref, other_m), (wide, other_g)))
    ]
    for copy in copies:
        copy.start()

    others = sums.at[pl.ds(0, etp_size - 1)]
    pltpu.make_async_copy(others, others, small_recv.at[0]).wait()
    group = sums[0]
    for n in range(1, etp_size):
        group = group + sums[n]
    totals[dp] = group

    if dp_size > 1:

        @pl.loop(1, dp_size)
        def _(step):
            pltpu.make_async_remote_copy(
                src_ref=totals.at[dp],
                dst_ref=totals.at[dp],
                send_sem=small_send.at[1],
                recv_sem=small_recv.at[1],
                device_id={"dp": lax.rem(dp + step, dp_size)},
                device_id_type=MESH,
            ).start()

        far = totals.at[pl.ds(0, dp_size - 1)]
        pltpu.make_async_copy(far, far, small_recv.at[1]).wait()
        pltpu.make_async_copy(far, far, small_send.at[1]).wait()
    pltpu.make_async_copy(others, others, small_send.at[0]).wait()
    everything = totals[0]
    for n in range(1, dp_size):
        everything = everything + totals[n]
    total_sq = jnp.sum(jnp.sum(everything, axis=0, keepdims=True), axis=1, keepdims=True)
    clip = jnp.minimum(1.0, lax.rsqrt(total_sq / element_count + epsilon))
    clip_out[...] = jnp.broadcast_to(clip, (8, BLOCK))
    for copy in copies:
        copy.wait()

    for b in range(BLOCKS):
        columns = slice(BLOCK * b, BLOCK * (b + 1))
        own = m_ref[:, columns] + clip * wide[:, columns]
        sib = other_m[:, columns] + clip * other_g[:, columns]
        blended = jnp.concatenate([own, sib], axis=0)
        for n, part in enumerate(split(blended, 2)):
            tall[b, :, BLOCK * n : BLOCK * (n + 1)] = part
        for n, part in enumerate(split(blended.T, 2)):
            flat[b, BLOCK * n : BLOCK * (n + 1), :] = part

    def place(chunk, of_core, s):
        tile = TILES * (2 * chunk + of_core) + s
        row = lax.rem(tile, BLOCKS)
        return row, lax.rem(row + tile // BLOCKS, BLOCKS)

    def own_tile(store, chunk, s):
        row, column = place(chunk, core, s)
        both = nn(flat[row], tall[column])
        part = lambda i, j: both[BLOCK * i : BLOCK * (i + 1), BLOCK * j : BLOCK * (j + 1)]
        store[s] = part(0, 0) + (part(0, 1) + (part(1, 0) + part(1, 1)))

    def at(steps):
        return lax.rem(chip + way * steps + RING, RING)

    half = BLOCK // HALVES
    halves = [(h, pl.ds(half * h, half)) for h in range(HALVES)]

    def remote(source, target, send, recv, device):
        return pltpu.make_async_remote_copy(
            src_ref=source,
            dst_ref=target,
            send_sem=send,
            recv_sem=recv,
            device_id={"etp": device},
            device_id_type=MESH,
        )

    def far_copy(step, s, h, rows):
        return remote(
            far_out.at[step, s, rows],
            far_in.at[step, s, rows],
            ring_send.at[0],
            far_recv.at[step, s, h],
            ahead,
        )

    def near_copy(step, s, h, rows):
        return remote(
            near_out.at[step, s, rows],
            near_in.at[step, s, rows],
            ring_send.at[1],
            near_recv.at[step, s, h],
            behind,
        )

    def gather_far(step, chunk, s, h, rows):
        place_of = tiles.at[chunk, s, rows]
        return remote(
            place_of, place_of, gather_send.at[0], gather_far_recv.at[step, s, h], ahead
        )

    def gather_near(step, chunk, s, h, rows):
        place_of = tiles.at[chunk, s, rows]
        return remote(
            place_of, place_of, gather_send.at[1], gather_near_recv.at[step, s, h], behind
        )

    def sib_copy(order, chunk, s, h, rows):
        return remote(
            tiles.at[chunk, s, rows],
            sib_tiles.at[chunk, s, rows],
            sib_send,
            sib_recv.at[order, s, h],
            sibling,
        )

    def expand(store, chunk, of_core, s):
        row, column = place(chunk, of_core, s)
        tile = store[chunk, s]
        for target, part in zip((w_high, w_mid), split(tile, 2)):
            target[row, column] = part
        for target, part in zip((w_high, w_mid), split(tile.T, 2)):
            target[column, row] = part

    def sib_expand(order, s):
        steps = 0 if order == 0 else (order + 1) // 2 if order % 2 else -(order // 2)
        for h, rows in halves:
            sib_copy(order, at(steps), s, h, rows).wait_recv()
        expand(sib_tiles, at(steps), 1 - core, s)

    @pl.loop(0, TILES)
    def _(s):
        own_tile(own_far, at(LONG), s)
        for h, rows in halves:
            far_out[0, s, rows] = own_far[s, rows]
            far_copy(0, s, h, rows).start()
        own_tile(own_near, at(-SHORT), s)
        for h, rows in halves:
            near_out[0, s, rows] = own_near[s, rows]
            near_copy(0, s, h, rows).start()

    @pl.loop(0, TILES)
    def _(s):
        own_tile(own_far, at(LONG - 1), s)
        own_tile(own_near, at(1 - SHORT), s)

    for step in range(1, LONG):

        @pl.loop(0, TILES)
        def _(s):
            for h, rows in halves:
                far_copy(step - 1, s, h, rows).wait_recv()
                far_out[step, s, rows] = own_far[s, rows] + far_in[step - 1, s, rows]
                far_copy(step, s, h, rows).start()
            own_tile(own_far, at(LONG - 1 - step), s)
            if step < SHORT:
                for h, rows in halves:
                    near_copy(step - 1, s, h, rows).wait_recv()
                    near_out[step, s, rows] = own_near[s, rows] + near_in[step - 1, s, rows]
                    near_copy(step, s, h, rows).start()
                if step < SHORT - 1:
                    own_tile(own_near, at(step + 1 - SHORT), s)

    @pl.loop(0, TILES)
    def _(s):
        for h, rows in halves:
            near_copy(SHORT - 1, s, h, rows).wait_recv()
            far_copy(LONG - 1, s, h, rows).wait_recv()
            tiles[chip, s, rows] = (
                own_far[s, rows] + near_in[SHORT - 1, s, rows] + far_in[LONG - 1, s, rows]
            )
            gather_far(0, chip, s, h, rows).start()
            gather_near(0, chip, s, h, rows).start()
            sib_copy(0, chip, s, h, rows).start()
        expand(tiles, chip, core, s)

    for step in range(LONG):

        @pl.loop(0, TILES)
        def _(s):
            from_behind, from_ahead = at(-1 - step), at(1 + step)
            for h, rows in halves:
                gather_far(step, from_behind, s, h, rows).wait_recv()
                if step < LONG - 1:
                    gather_far(step + 1, from_behind, s, h, rows).start()
                sib_copy(2 * step + 1, from_behind, s, h, rows).start()
            expand(tiles, from_behind, core, s)
            if step < SHORT:
                for h, rows in halves:
                    gather_near(step, from_ahead, s, h, rows).wait_recv()
                    if step < SHORT - 1:
                        gather_near(step + 1, from_ahead, s, h, rows).start()
                    sib_copy(2 * step + 2, from_ahead, s, h, rows).start()
                expand(tiles, from_ahead, core, s)
            for order in range(max(0, 2 * step - 1), 2 * step + 1):
                sib_expand(order, s)

    @pl.loop(0, TILES)
    def _(s):
        sib_expand(RING - 1, s)

    def keep(values, target):
        for n, part in enumerate(split(values, 3)):
            target[RANK * n : RANK * (n + 1), :] = part

    def gram_columns(terms, n):
        def weights(store):
            return jnp.concatenate(
                [
                    jnp.concatenate([store[i, 2 * n], store[i, 2 * n + 1]], axis=1)
                    for i in range(BLOCKS)
                ],
                axis=0,
            )

        first = nn(terms[...], weights(w_high))
        second = nn(terms[: 2 * RANK, :], weights(w_mid))
        v_ref[:, 2 * BLOCK * n : 2 * BLOCK * (n + 1)] = first[:RANK] + (
            (first[RANK : 2 * RANK] + second[:RANK]) + (first[2 * RANK :] + second[RANK:])
        )

    def small_gram():
        both = nt(r_terms[...], z_terms[...])
        part = lambda i, j: both[RANK * i : RANK * (i + 1), RANK * j : RANK * (j + 1)]
        return part(0, 0) + (
            (part(0, 1) + part(1, 0)) + (part(1, 1) + (part(0, 2) + part(2, 0)))
        )

    def apply(inverse, terms):
        high, middle, low = split(inverse, 3)
        none = jnp.zeros_like(high)
        stack = jnp.concatenate(
            [
                jnp.concatenate([high, high, high], axis=1),
                jnp.concatenate([middle, middle, none], axis=1),
                jnp.concatenate([low, none, none], axis=1),
            ],
            axis=0,
        )
        result = nn(stack, terms[...])
        return result[:RANK] + (result[RANK : 2 * RANK] + result[2 * RANK :])

    def normalise(across):
        return lax.rsqrt(jnp.sum(across * across, axis=1, keepdims=True) + epsilon)

    keep(q_ref[...], r_terms)

    @pl.loop(0, DIRECT)
    def _(turn):
        for n in range(BLOCKS // 2):
            gram_columns(r_terms, n)
        keep(v_ref[...], z_terms)
        inverse = inverse_cholesky(small_gram())
        across = apply(inverse, z_terms)
        keep(across * normalise(across), r_terms)

    for n in range(BLOCKS // 2):
        gram_columns(r_terms, n)
    keep(v_ref[...], z_terms)

    @pl.loop(DIRECT, ITERS - 1)
    def _(turn):
        inverse = inverse_cholesky(
            small_gram(),
            [functools.partial(gram_columns, z_terms, n) for n in range(BLOCKS // 2)],
        )
        keep(v_ref[...], v_terms)
        across = apply(inverse, z_terms)
        ahead_of = apply(inverse, v_terms)
        scale = normalise(across)
        keep(across * scale, r_terms)
        keep(ahead_of * scale, z_terms)

    inverse = inverse_cholesky(small_gram())
    across = apply(inverse, z_terms)
    scale = normalise(across)
    r_out[...] = across * scale
    left_map = apply(inverse, r_terms)
    norm = scale * (jnp.sum(across * across, axis=1, keepdims=True) + epsilon)
    maps = jnp.concatenate(split(left_map * norm, 2) + split(left_map, 2), axis=0)
    blended = m_ref[...] + clip * wide[...]
    both = nt(jnp.concatenate(split(blended, 2), axis=0), maps)
    both = both[:rows] + both[rows:]
    for n in range(2):
        first = both[:, 2 * RANK * n : 2 * RANK * n + RANK]
        left_out[:, RANK * n : RANK * (n + 1)] = (
            first + both[:, 2 * RANK * n + RANK : 2 * RANK * (n + 1)]
        )

    for sent, semaphore in (
        (far_out, ring_send.at[0]),
        (near_out, ring_send.at[1]),
        (tiles.at[pl.ds(0, LONG)], gather_send.at[0]),
        (tiles.at[pl.ds(0, SHORT)], gather_send.at[1]),
        (tiles, sib_send),
    ):
        pltpu.make_async_copy(sent, sent, semaphore).wait()


def finish_kernel(m_ref, g_ref, clip_ref, left_ref, r_ref, m_out, q_out, u_out):
    blended = m_ref[...] + clip_ref[0:1, 0:1] * g_ref[...].astype(F32)
    rows = blended.shape[0]
    left = jnp.concatenate([left_ref[:, :RANK], left_ref[:, RANK:]], axis=0)
    high, middle = split(left, 2)
    right = split(r_ref[...], 2)
    outer = nn(
        jnp.concatenate([high, high, middle, middle], axis=1),
        jnp.concatenate(right + right, axis=0),
    )
    m_out[...] = blended - (1.0 - keep_rate) * outer[:rows]
    update_scale = math.sqrt(ROWS * COLS / RANK)
    u_out[...] = (update_scale * outer[rows:]).astype(BF16)
    q_out[...] = r_ref[...]


def body(momentum, grad, q_in):
    dp_size = lax.axis_size("dp")
    rows, cols = momentum.shape[1:]
    element_count = float(dp_size * rows * 2 * RING * cols)
    m, g, q = momentum[0], grad[0], q_in[0].T
    vmem = pl.BlockSpec(memory_space=pltpu.VMEM)
    hbm = pl.BlockSpec(memory_space=pl.ANY)
    tile = (BLOCK, BLOCK)
    dma = pltpu.SemaphoreType.DMA
    left, r_t, clip = pl.pallas_call(
        functools.partial(refresh_kernel, dp_size, element_count),
        out_shape=[
            jax.ShapeDtypeStruct((rows, 2 * RANK), F32),
            jax.ShapeDtypeStruct((RANK, cols), F32),
            jax.ShapeDtypeStruct((8, BLOCK), F32),
        ],
        in_specs=[hbm] * 3,
        out_specs=[vmem] * 3,
        scratch_shapes=[
            pltpu.VMEM((rows, cols), F32),
            pltpu.VMEM((rows, cols), BF16),
            pltpu.VMEM((RANK, cols), F32),
            pltpu.VMEM((rows, cols), F32),
            pltpu.VMEM((rows, cols), F32),
            pltpu.VMEM((rows, cols), F32),
            pltpu.VMEM((2 * RING, 8, BLOCK), F32),
            pltpu.VMEM((dp_size, 8, BLOCK), F32),
            pltpu.VMEM((BLOCKS, 2 * rows, 2 * BLOCK), BF16),
            pltpu.VMEM((BLOCKS, 2 * BLOCK, 2 * rows), BF16),
            pltpu.VMEM((TILES,) + tile, F32),
            pltpu.VMEM((TILES,) + tile, F32),
            pltpu.VMEM((LONG, TILES) + tile, F32),
            pltpu.VMEM((LONG, TILES) + tile, F32),
            pltpu.VMEM((SHORT, TILES) + tile, F32),
            pltpu.VMEM((SHORT, TILES) + tile, F32),
            pltpu.VMEM((RING, TILES) + tile, F32),
            pltpu.VMEM((RING, TILES) + tile, F32),
            pltpu.VMEM((BLOCKS, BLOCKS) + tile, BF16),
            pltpu.VMEM((BLOCKS, BLOCKS) + tile, BF16),
            pltpu.VMEM((3 * RANK, cols), BF16),
            pltpu.VMEM((3 * RANK, cols), BF16),
            pltpu.VMEM((3 * RANK, cols), BF16),
            pltpu.VMEM((RANK, cols), F32),
            dma((3,)),
            dma((2,)),
            dma((2,)),
            dma((2,)),
            dma((2,)),
            dma((2,)),
            dma((LONG, TILES, HALVES)),
            dma((SHORT, TILES, HALVES)),
            dma((2,)),
            dma((LONG, TILES, HALVES)),
            dma((SHORT, TILES, HALVES)),
            dma,
            dma((RING, TILES, HALVES)),
        ],
        compiler_params=pltpu.CompilerParams(
            collective_id=0, has_side_effects=True, vmem_limit_bytes=56 << 20
        ),
    )(m, g, q)
    part = rows // 2
    whole = lambda shape: pl.BlockSpec(shape, lambda n: (0, 0))
    by_rows = pl.BlockSpec((part, cols), lambda n: (n, 0))
    m_new, q_new, update = pl.pallas_call(
        finish_kernel,
        grid=(2,),
        out_shape=[
            jax.ShapeDtypeStruct((rows, cols), F32),
            jax.ShapeDtypeStruct((RANK, cols), F32),
            jax.ShapeDtypeStruct((rows, cols), BF16),
        ],
        in_specs=[
            by_rows,
            by_rows,
            whole((8, BLOCK)),
            pl.BlockSpec((part, 2 * RANK), lambda n: (n, 0)),
            whole((RANK, cols)),
        ],
        out_specs=[by_rows, whole((RANK, cols)), by_rows],
        compiler_params=pltpu.CompilerParams(vmem_limit_bytes=24 << 20),
    )(m, g, clip, left, r_t)
    return m_new[None], q_new.T[None], update[None]


def solution(mesh):
    return jax.shard_map(
        body,
        mesh=mesh,
        in_specs=(P("dp", "etp", None), P("dp", "etp", None), P("dp", None, None)),
        out_specs=(P("dp", "etp", None), P("dp", None, None), P("dp", "etp", None)),
        check_vma=False,
    )
```

```python
import functools
import math

import jax
import jax.numpy as jnp
from jax import lax
from jax.experimental import pallas as pl
from jax.experimental.pallas import tpu as pltpu
from jax.sharding import PartitionSpec as P

ROWS = 3584
COLS = 1536
RANK = 64
ITERS = 8
DIRECT = 3

BLOCK = 128
BLOCKS = COLS // BLOCK
SLOTS = 9
SLOT = BLOCK + 8
CHUNK = 4 * BLOCK + 8 + BLOCK // 2
RING = 8
LONG = RING // 2
SHORT = RING - 1 - LONG

LAST, HALF = "last", "half"

keep_rate = 0.9
epsilon = 1e-06

MESH = pl.DeviceIdType.MESH
F32 = jnp.float32
BF16 = jnp.bfloat16


def nn(former, latter):
    return jnp.dot(former, latter, preferred_element_type=F32)


def nt(former, latter):
    return lax.dot_general(former, latter, (((1,), (1,)), ((), ())), preferred_element_type=F32)


def split(values, terms):
    parts = []
    for _ in range(terms):
        parts.append(values.astype(BF16))
        values = values - parts[-1].astype(F32)
    return parts


def inverse_cholesky(gram, between=()):
    full = (8, 2 * RANK)
    ones = lax.broadcasted_iota(jnp.int32, (RANK, RANK), 0) == lax.broadcasted_iota(
        jnp.int32, (RANK, RANK), 1
    )
    joined = jnp.concatenate([gram, ones.astype(F32)], axis=1)
    panels = [joined[8 * p : 8 * p + 8] for p in range(RANK // 8)]
    sublane = lax.broadcasted_iota(jnp.int32, full, 0)
    for p in range(RANK // 8):
        if p < len(between):
            between[p]()
        panel = panels[p]
        entry = [[None] * 8 for _ in range(8)]
        for i in range(8):
            for j in range(i + 1):
                entry[i][j] = jnp.broadcast_to(panel[i : i + 1, 8 * p + j : 8 * p + j + 1], full)
        rows = [jnp.broadcast_to(panel[i : i + 1, :], full) for i in range(8)]
        scale = [None] * 8
        factor = [[None] * 8 for _ in range(8)]
        for j in range(8):
            scale[j] = lax.rsqrt(entry[j][j])
            for i in range(j + 1, 8):
                factor[i][j] = entry[i][j] * scale[j]
            for i in range(j + 1, 8):
                for m in range(j + 1, i + 1):
                    entry[i][m] = entry[i][m] - factor[i][j] * factor[m][j]
            rows[j] = rows[j] * scale[j]
            for i in range(j + 1, 8):
                rows[i] = rows[i] - factor[i][j] * rows[j]
        done = rows[0]
        for i in range(1, 8):
            done = jnp.where(sublane == i, rows[i], done)
        panels[p] = done
        for q in range(p + 1, RANK // 8):
            column = [
                jnp.broadcast_to(panels[q][:, 8 * p + j : 8 * p + j + 1], full) for j in range(8)
            ]
            for j in range(8):
                column[j] = column[j] * scale[j]
                for i in range(j + 1, 8):
                    column[i] = column[i] - factor[i][j] * column[j]
            left = panels[q]
            for j in range(8):
                left = left - column[j] * rows[j]
            panels[q] = left
    return jnp.concatenate(panels, axis=0)[:, RANK:]


def refresh_kernel(
    dp_size,
    element_count,
    m_hbm,
    g_hbm,
    q_hbm,
    left_out,
    r_out,
    clip_out,
    m_ref,
    g_ref,
    q_ref,
    wide,
    other_m,
    other_g,
    sums,
    totals,
    tall,
    flat,
    own_far,
    own_near,
    far_in,
    far_out,
    near_in,
    near_out,
    tiles,
    w_high,
    w_mid,
    r_terms,
    z_terms,
    v_terms,
    v_ref,
    load,
    small_send,
    small_recv,
    big_send,
    big_recv,
    ring_send,
    far_recv,
    near_recv,
    gather_send,
    gather_far_recv,
    gather_near_recv,
    sib_send,
    sib_recv,
):
    me = lax.axis_index("etp")
    dp = lax.axis_index("dp")
    etp_size = 2 * RING
    chip = me // 2
    core = lax.rem(me, 2)
    sibling = chip * 2 + (1 - core)
    way = 1 - 2 * core
    ahead = lax.rem(chip + way + RING, RING) * 2 + core
    behind = lax.rem(chip - way + RING, RING) * 2 + core
    rows = m_ref.shape[0]

    barrier = pltpu.get_barrier_semaphore()

    @pl.loop(1, etp_size)
    def _(step):
        pl.semaphore_signal(
            barrier, inc=1, device_id={"etp": lax.rem(me + step, etp_size)}, device_id_type=MESH
        )

    @pl.loop(1, dp_size)
    def _(step):
        pl.semaphore_signal(
            barrier, inc=1, device_id={"dp": lax.rem(dp + step, dp_size)}, device_id_type=MESH
        )

    loads = [
        pltpu.make_async_copy(source, target, load.at[n])
        for n, (source, target) in enumerate(((g_hbm, g_ref), (m_hbm, m_ref), (q_hbm, q_ref)))
    ]
    for copy in loads:
        copy.start()
    loads[0].wait()
    wide[...] = g_ref[...].astype(F32)
    partial = jnp.zeros((8, BLOCK), F32)
    for b in range(BLOCKS):
        piece = wide[:, BLOCK * b : BLOCK * (b + 1)]
        partial = partial + jnp.sum((piece * piece).reshape(rows // 8, 8, BLOCK), axis=0)
    sums[me] = partial
    loads[1].wait()
    loads[2].wait()

    pl.semaphore_wait(barrier, etp_size + dp_size - 2)

    @pl.loop(1, etp_size)
    def _(step):
        pltpu.make_async_remote_copy(
            src_ref=sums.at[me],
            dst_ref=sums.at[me],
            send_sem=small_send.at[0],
            recv_sem=small_recv.at[0],
            device_id={"etp": lax.rem(me + step, etp_size)},
            device_id_type=MESH,
        ).start()

    copies = [
        pltpu.make_async_remote_copy(
            src_ref=source,
            dst_ref=target,
            send_sem=big_send.at[n],
            recv_sem=big_recv.at[n],
            device_id={"etp": sibling},
            device_id_type=MESH,
        )
        for n, (source, target) in enumerate(((m_ref, other_m), (wide, other_g)))
    ]
    for copy in copies:
        copy.start()

    others = sums.at[pl.ds(0, etp_size - 1)]
    pltpu.make_async_copy(others, others, small_recv.at[0]).wait()
    group = sums[0]
    for n in range(1, etp_size):
        group = group + sums[n]
    totals[dp] = group

    if dp_size > 1:

        @pl.loop(1, dp_size)
        def _(step):
            pltpu.make_async_remote_copy(
                src_ref=totals.at[dp],
                dst_ref=totals.at[dp],
                send_sem=small_send.at[1],
                recv_sem=small_recv.at[1],
                device_id={"dp": lax.rem(dp + step, dp_size)},
                device_id_type=MESH,
            ).start()

        far = totals.at[pl.ds(0, dp_size - 1)]
        pltpu.make_async_copy(far, far, small_recv.at[1]).wait()
        pltpu.make_async_copy(far, far, small_send.at[1]).wait()
    pltpu.make_async_copy(others, others, small_send.at[0]).wait()
    everything = totals[0]
    for n in range(1, dp_size):
        everything = everything + totals[n]
    total_sq = jnp.sum(jnp.sum(everything, axis=0, keepdims=True), axis=1, keepdims=True)
    clip = jnp.minimum(1.0, lax.rsqrt(total_sq / element_count + epsilon))
    clip_out[...] = jnp.broadcast_to(clip, (8, BLOCK))
    for copy in copies:
        copy.wait()

    for b in range(BLOCKS):
        columns = slice(BLOCK * b, BLOCK * (b + 1))
        own = m_ref[:, columns] + clip * wide[:, columns]
        sib = other_m[:, columns] + clip * other_g[:, columns]
        blended = jnp.concatenate([own, sib], axis=0)
        for n, part in enumerate(split(blended, 2)):
            tall[b, :, BLOCK * n : BLOCK * (n + 1)] = part
        for n, part in enumerate(split(blended.T, 2)):
            flat[b, BLOCK * n : BLOCK * (n + 1), :] = part

    def place(chunk, slot):
        tile = RING * slot + chunk
        row = lax.rem(tile, BLOCKS)
        return row, lax.rem(row + tile // BLOCKS + 1, BLOCKS)

    def is_pair(chunk, of_core):
        return of_core * ((chunk + 6) // RING)

    tile_row = lax.broadcasted_iota(jnp.int32, (BLOCK, BLOCK), 0)
    tile_column = lax.broadcasted_iota(jnp.int32, (BLOCK, BLOCK), 1)

    def product(row, column):
        both = nn(flat[row], tall[column])
        part = lambda i, j: both[BLOCK * i : BLOCK * (i + 1), BLOCK * j : BLOCK * (j + 1)]
        return part(0, 0) + (part(0, 1) + (part(1, 0) + part(1, 1)))

    def own_terms(store, chunk, s):
        if s is LAST:
            pair = is_pair(chunk, core)
            row, column = place(chunk, 3 + 5 * core)
            first = product(
                pair * (chunk - 2) + (1 - pair) * row, pair * (chunk - 2) + (1 - pair) * column
            )
            second = product(
                pair * (chunk + 4) + (1 - pair) * row, pair * (chunk + 4) + (1 - pair) * column
            )
            store[3 * BLOCK : 4 * BLOCK] = jnp.where(
                tile_row + (1 - pair) * BLOCK >= tile_column, first, second
            )
            diagonal = jnp.sum(
                jnp.where(tile_row == tile_column, second, 0.0), axis=0, keepdims=True
            )
            store[4 * BLOCK : 4 * BLOCK + 8] = jnp.broadcast_to(diagonal, (8, BLOCK))
        elif s is HALF:
            row, column = place(chunk, 4)
            start = pl.multiple_of(core * (BLOCK // 2), BLOCK // 2)
            rows_of = [flat[row, pl.ds(BLOCK * n + start, BLOCK // 2)] for n in range(2)]
            both = nn(jnp.concatenate(rows_of, axis=0), tall[column])
            upper, lower = both[: BLOCK // 2], both[BLOCK // 2 :]
            store[CHUNK - BLOCK // 2 :] = upper[:, :BLOCK] + (
                upper[:, BLOCK:] + (lower[:, :BLOCK] + lower[:, BLOCK:])
            )
        else:
            row, column = place(chunk, s + 5 * core)
            store[pl.ds(pl.multiple_of(BLOCK * s, BLOCK), BLOCK)] = product(row, column)

    def at(steps):
        return lax.rem(chip + way * steps + RING, RING)

    def index(s):
        return 3 if s is LAST else 4 if s is HALF else s

    def part_of(s):
        if s is LAST:
            return pl.ds(3 * BLOCK, SLOT)
        if s is HALF:
            return pl.ds(CHUNK - BLOCK // 2, BLOCK // 2)
        return pl.ds(pl.multiple_of(BLOCK * s, BLOCK), BLOCK)

    def slot_rows(slot, size=BLOCK):
        return pl.ds(pl.multiple_of(SLOT * slot, 8), size)

    def finished(chunk, of_core, s):
        if s is HALF:
            start = pl.multiple_of(4 * SLOT + of_core * (BLOCK // 2), 8)
            return tiles.at[chunk, pl.ds(start, BLOCK // 2)]
        return tiles.at[chunk, slot_rows(index(s) + 5 * of_core, SLOT if s is LAST else BLOCK)]

    def each(visit):
        @pl.loop(0, 3)
        def _(s):
            visit(s)

        visit(LAST)
        visit(HALF)

    def remote(source, target, send, recv, device):
        return pltpu.make_async_remote_copy(
            src_ref=source,
            dst_ref=target,
            send_sem=send,
            recv_sem=recv,
            device_id={"etp": device},
            device_id_type=MESH,
        )

    def far_copy(step, s):
        return remote(
            far_out.at[step, part_of(s)],
            far_in.at[step, part_of(s)],
            ring_send.at[0],
            far_recv.at[step, index(s)],
            ahead,
        )

    def near_copy(step, s):
        return remote(
            near_out.at[step, part_of(s)],
            near_in.at[step, part_of(s)],
            ring_send.at[1],
            near_recv.at[step, index(s)],
            behind,
        )

    def gather_far(step, chunk, s):
        view = finished(chunk, core, s)
        return remote(view, view, gather_send.at[0], gather_far_recv.at[step, index(s)], ahead)

    def gather_near(step, chunk, s):
        view = finished(chunk, core, s)
        return remote(view, view, gather_send.at[1], gather_near_recv.at[step, index(s)], behind)

    def sib_copy(order, chunk, of_core, s):
        view = finished(chunk, of_core, s)
        return remote(view, view, sib_send, sib_recv.at[order, index(s)], sibling)

    def store_tile(row, column, tile):
        for target, part in zip((w_high, w_mid), split(tile, 2)):
            target[row, column] = part

    def expand_slot(chunk, slot):
        row, column = place(chunk, slot)
        tile = tiles[chunk, slot_rows(slot)]
        store_tile(row, column, tile)
        store_tile(column, row, tile.T)

    def expand(chunk, of_core, s):
        if s is not LAST:
            expand_slot(chunk, s + 5 * of_core)
            return
        pair = is_pair(chunk, of_core)
        slot = 3 + 5 * of_core

        @pl.when(pair == 0)
        def _():
            expand_slot(chunk, slot)

        @pl.when(pair == 1)
        def _():
            tile = tiles[chunk, slot_rows(slot)]
            turned = tile.T
            start = pl.multiple_of(SLOT * slot + BLOCK, 8)
            diagonal = jnp.broadcast_to(tiles[chunk, pl.ds(start, 8)][0:1], (BLOCK, BLOCK))
            store_tile(chunk - 2, chunk - 2, jnp.where(tile_row >= tile_column, tile, turned))
            other = jnp.where(tile_row == tile_column, diagonal, turned)
            store_tile(
                chunk + 4, chunk + 4, jnp.where(tile_row < tile_column, tile, other)
            )

    def sib_expand(order, s):
        steps = 0 if order == 0 else (order + 1) // 2 if order % 2 else -(order // 2)
        sib_copy(order, at(steps), 1 - core, s).wait_recv()
        if s is HALF:
            expand_slot(at(steps), 4)
        else:
            expand(at(steps), 1 - core, s)

    def start_ring(s):
        own_terms(own_far, at(LONG), s)
        far_out[0, part_of(s)] = own_far[part_of(s)]
        far_copy(0, s).start()
        own_terms(own_near, at(-SHORT), s)
        near_out[0, part_of(s)] = own_near[part_of(s)]
        near_copy(0, s).start()

    def next_terms(s):
        own_terms(own_far, at(LONG - 1), s)
        own_terms(own_near, at(1 - SHORT), s)

    each(start_ring)
    each(next_terms)

    def pass_on(step, s):
        rows = part_of(s)
        far_copy(step - 1, s).wait_recv()
        far_out[step, rows] = own_far[rows] + far_in[step - 1, rows]
        far_copy(step, s).start()
        if step < SHORT:
            near_copy(step - 1, s).wait_recv()
            near_out[step, rows] = own_near[rows] + near_in[step - 1, rows]
            near_copy(step, s).start()
        own_terms(own_far, at(LONG - 1 - step), s)
        if step < SHORT - 1:
            own_terms(own_near, at(step + 1 - SHORT), s)

    for step in range(1, LONG):
        each(functools.partial(pass_on, step))

    def finish_sum(s):
        rows = part_of(s)
        near_copy(SHORT - 1, s).wait_recv()
        far_copy(LONG - 1, s).wait_recv()
        view = finished(chip, core, s)
        view[...] = own_far[rows] + near_in[SHORT - 1, rows] + far_in[LONG - 1, rows]
        gather_far(0, chip, s).start()
        gather_near(0, chip, s).start()
        sib_copy(0, chip, core, s).start()
        if s is not HALF:
            expand(chip, core, s)

    each(finish_sum)

    def spread(step, s):
        from_behind, from_ahead = at(-1 - step), at(1 + step)
        gather_far(step, from_behind, s).wait_recv()
        if step < LONG - 1:
            gather_far(step + 1, from_behind, s).start()
        sib_copy(2 * step + 1, from_behind, core, s).start()
        if step < SHORT:
            gather_near(step, from_ahead, s).wait_recv()
            if step < SHORT - 1:
                gather_near(step + 1, from_ahead, s).start()
            sib_copy(2 * step + 2, from_ahead, core, s).start()
        if s is not HALF:
            expand(from_behind, core, s)
            if step < SHORT:
                expand(from_ahead, core, s)
        for order in range(max(0, 2 * step - 1), 2 * step + 1):
            sib_expand(order, s)

    for step in range(LONG):
        each(functools.partial(spread, step))

    each(functools.partial(sib_expand, RING - 1))

    def keep(values, target):
        for n, part in enumerate(split(values, 3)):
            target[RANK * n : RANK * (n + 1), :] = part

    def gram_columns(terms, n):
        def weights(store):
            return jnp.concatenate(
                [
                    jnp.concatenate([store[i, 2 * n], store[i, 2 * n + 1]], axis=1)
                    for i in range(BLOCKS)
                ],
                axis=0,
            )

        first = nn(terms[...], weights(w_high))
        second = nn(terms[: 2 * RANK, :], weights(w_mid))
        v_ref[:, 2 * BLOCK * n : 2 * BLOCK * (n + 1)] = first[:RANK] + (
            (first[RANK : 2 * RANK] + second[:RANK]) + (first[2 * RANK :] + second[RANK:])
        )

    def small_gram():
        both = nt(r_terms[...], z_terms[...])
        part = lambda i, j: both[RANK * i : RANK * (i + 1), RANK * j : RANK * (j + 1)]
        return part(0, 0) + (
            (part(0, 1) + part(1, 0)) + (part(1, 1) + (part(0, 2) + part(2, 0)))
        )

    def apply(inverse, terms):
        high, middle, low = split(inverse, 3)
        none = jnp.zeros_like(high)
        stack = jnp.concatenate(
            [
                jnp.concatenate([high, high, high], axis=1),
                jnp.concatenate([middle, middle, none], axis=1),
                jnp.concatenate([low, none, none], axis=1),
            ],
            axis=0,
        )
        result = nn(stack, terms[...])
        return result[:RANK] + (result[RANK : 2 * RANK] + result[2 * RANK :])

    def normalise(across):
        return lax.rsqrt(jnp.sum(across * across, axis=1, keepdims=True) + epsilon)

    keep(q_ref[...], r_terms)

    @pl.loop(0, DIRECT)
    def _(turn):
        for n in range(BLOCKS // 2):
            gram_columns(r_terms, n)
        keep(v_ref[...], z_terms)
        inverse = inverse_cholesky(small_gram())
        across = apply(inverse, z_terms)
        keep(across * normalise(across), r_terms)

    for n in range(BLOCKS // 2):
        gram_columns(r_terms, n)
    keep(v_ref[...], z_terms)

    @pl.loop(DIRECT, ITERS - 1)
    def _(turn):
        inverse = inverse_cholesky(
            small_gram(),
            [functools.partial(gram_columns, z_terms, n) for n in range(BLOCKS // 2)],
        )
        keep(v_ref[...], v_terms)
        across = apply(inverse, z_terms)
        ahead_of = apply(inverse, v_terms)
        scale = normalise(across)
        keep(across * scale, r_terms)
        keep(ahead_of * scale, z_terms)

    inverse = inverse_cholesky(small_gram())
    across = apply(inverse, z_terms)
    scale = normalise(across)
    r_out[...] = across * scale
    left_map = apply(inverse, r_terms)
    norm = scale * (jnp.sum(across * across, axis=1, keepdims=True) + epsilon)
    maps = jnp.concatenate(split(left_map * norm, 2) + split(left_map, 2), axis=0)
    blended = m_ref[...] + clip * wide[...]
    both = nt(jnp.concatenate(split(blended, 2), axis=0), maps)
    both = both[:rows] + both[rows:]
    for n in range(2):
        first = both[:, 2 * RANK * n : 2 * RANK * n + RANK]
        left_out[:, RANK * n : RANK * (n + 1)] = (
            first + both[:, 2 * RANK * n + RANK : 2 * RANK * (n + 1)]
        )

    for sent, semaphore in (
        (far_out, ring_send.at[0]),
        (near_out, ring_send.at[1]),
        (far_out, gather_send.at[0]),
        (near_out, gather_send.at[1]),
        (tiles.at[:, pl.ds(0, CHUNK)], sib_send),
    ):
        pltpu.make_async_copy(sent, sent, semaphore).wait()


def finish_kernel(m_ref, g_ref, clip_ref, left_ref, r_ref, m_out, q_out, u_out):
    blended = m_ref[...] + clip_ref[0:1, 0:1] * g_ref[...].astype(F32)
    rows = blended.shape[0]
    left = jnp.concatenate([left_ref[:, :RANK], left_ref[:, RANK:]], axis=0)
    high, middle = split(left, 2)
    right = split(r_ref[...], 2)
    outer = nn(
        jnp.concatenate([high, high, middle, middle], axis=1),
        jnp.concatenate(right + right, axis=0),
    )
    m_out[...] = blended - (1.0 - keep_rate) * outer[:rows]
    update_scale = math.sqrt(ROWS * COLS / RANK)
    u_out[...] = (update_scale * outer[rows:]).astype(BF16)
    q_out[...] = r_ref[...]


def body(momentum, grad, q_in):
    dp_size = lax.axis_size("dp")
    rows, cols = momentum.shape[1:]
    element_count = float(dp_size * rows * 2 * RING * cols)
    m, g, q = momentum[0], grad[0], q_in[0].T
    vmem = pl.BlockSpec(memory_space=pltpu.VMEM)
    hbm = pl.BlockSpec(memory_space=pl.ANY)
    tile = (BLOCK, BLOCK)
    dma = pltpu.SemaphoreType.DMA
    left, r_t, clip = pl.pallas_call(
        functools.partial(refresh_kernel, dp_size, element_count),
        out_shape=[
            pltpu.VMEM((rows, 2 * RANK), F32),
            pltpu.VMEM((RANK, cols), F32),
            pltpu.VMEM((8, BLOCK), F32),
        ],
        in_specs=[hbm] * 3,
        out_specs=[vmem] * 3,
        scratch_shapes=[
            pltpu.VMEM((rows, cols), F32),
            pltpu.VMEM((rows, cols), BF16),
            pltpu.VMEM((RANK, cols), F32),
            pltpu.VMEM((rows, cols), F32),
            pltpu.VMEM((rows, cols), F32),
            pltpu.VMEM((rows, cols), F32),
            pltpu.VMEM((2 * RING, 8, BLOCK), F32),
            pltpu.VMEM((dp_size, 8, BLOCK), F32),
            pltpu.VMEM((BLOCKS, 2 * rows, 2 * BLOCK), BF16),
            pltpu.VMEM((BLOCKS, 2 * BLOCK, 2 * rows), BF16),
            pltpu.VMEM((CHUNK, BLOCK), F32),
            pltpu.VMEM((CHUNK, BLOCK), F32),
            pltpu.VMEM((LONG, CHUNK, BLOCK), F32),
            pltpu.VMEM((LONG, CHUNK, BLOCK), F32),
            pltpu.VMEM((SHORT, CHUNK, BLOCK), F32),
            pltpu.VMEM((SHORT, CHUNK, BLOCK), F32),
            pltpu.VMEM((RING, SLOTS * SLOT, BLOCK), F32),
            pltpu.VMEM((BLOCKS, BLOCKS) + tile, BF16),
            pltpu.VMEM((BLOCKS, BLOCKS) + tile, BF16),
            pltpu.VMEM((3 * RANK, cols), BF16),
            pltpu.VMEM((3 * RANK, cols), BF16),
            pltpu.VMEM((3 * RANK, cols), BF16),
            pltpu.VMEM((RANK, cols), F32),
            dma((3,)),
            dma((2,)),
            dma((2,)),
            dma((2,)),
            dma((2,)),
            dma((2,)),
            dma((LONG, 5)),
            dma((SHORT, 5)),
            dma((2,)),
            dma((LONG, 5)),
            dma((SHORT, 5)),
            dma,
            dma((RING, 5)),
        ],
        compiler_params=pltpu.CompilerParams(
            collective_id=0, has_side_effects=True, vmem_limit_bytes=56 << 20
        ),
    )(m, g, q)
    part = rows // 2
    whole = lambda shape: pl.BlockSpec(shape, lambda n: (0, 0))
    by_rows = pl.BlockSpec((part, cols), lambda n: (n, 0))
    m_new, q_new, update = pl.pallas_call(
        finish_kernel,
        grid=(2,),
        out_shape=[
            jax.ShapeDtypeStruct((rows, cols), F32),
            jax.ShapeDtypeStruct((RANK, cols), F32),
            jax.ShapeDtypeStruct((rows, cols), BF16),
        ],
        in_specs=[
            by_rows,
            by_rows,
            whole((8, BLOCK)),
            pl.BlockSpec((part, 2 * RANK), lambda n: (n, 0)),
            whole((RANK, cols)),
        ],
        out_specs=[by_rows, whole((RANK, cols)), by_rows],
        compiler_params=pltpu.CompilerParams(vmem_limit_bytes=24 << 20),
    )(m, g, clip, left, r_t)
    return m_new[None], q_new.T[None], update[None]


def solution(mesh):
    return jax.shard_map(
        body,
        mesh=mesh,
        in_specs=(P("dp", "etp", None), P("dp", "etp", None), P("dp", None, None)),
        out_specs=(P("dp", "etp", None), P("dp", None, None), P("dp", "etp", None)),
        check_vma=False,
    )
```

```python
import functools
import math

import jax
import jax.numpy as jnp
from jax import lax
from jax.experimental import pallas as pl
from jax.experimental.pallas import tpu as pltpu
from jax.sharding import PartitionSpec as P

ROWS = 3584
COLS = 1536
RANK = 64
ITERS = 8
DIRECT = 3

BLOCK = 128
BLOCKS = COLS // BLOCK
SLOTS = 9
SLOT = BLOCK + 8
CHUNK = 4 * BLOCK + 8 + BLOCK // 2
RING = 8
LONG = RING // 2
SHORT = RING - 1 - LONG

LAST, HALF = "last", "half"

keep_rate = 0.9
epsilon = 1e-06

MESH = pl.DeviceIdType.MESH
F32 = jnp.float32
BF16 = jnp.bfloat16


def nn(former, latter):
    return jnp.dot(former, latter, preferred_element_type=F32)


def nt(former, latter):
    return lax.dot_general(former, latter, (((1,), (1,)), ((), ())), preferred_element_type=F32)


def split(values, terms):
    parts = []
    for _ in range(terms):
        parts.append(values.astype(BF16))
        values = values - parts[-1].astype(F32)
    return parts


def inverse_cholesky(gram, lines, between=()):
    full = (8, 2 * RANK)
    ones = lax.broadcasted_iota(jnp.int32, (RANK, RANK), 0) == lax.broadcasted_iota(
        jnp.int32, (RANK, RANK), 1
    )
    joined = jnp.concatenate([gram, ones.astype(F32)], axis=1)
    panels = [joined[8 * p : 8 * p + 8] for p in range(RANK // 8)]
    sublane = lax.broadcasted_iota(jnp.int32, full, 0)
    for p in range(RANK // 8):
        if p < len(between):
            between[p]()
        lines[p] = panels[p]
        rows = [jnp.broadcast_to(lines[p, i : i + 1, :], full) for i in range(8)]
        entry = [[None] * 8 for _ in range(8)]
        for j in range(8):
            own = RANK // 8 + 8 * p + j
            lines[own] = jnp.broadcast_to(panels[p][:, 8 * p + j : 8 * p + j + 1], full)
            for i in range(j, 8):
                entry[i][j] = jnp.broadcast_to(lines[own, i : i + 1, :], full)
        scale = [None] * 8
        factor = [[None] * 8 for _ in range(8)]
        for j in range(8):
            scale[j] = lax.rsqrt(entry[j][j])
            for i in range(j + 1, 8):
                factor[i][j] = entry[i][j] * scale[j]
            for i in range(j + 1, 8):
                for m in range(j + 1, i + 1):
                    entry[i][m] = entry[i][m] - factor[i][j] * factor[m][j]
            rows[j] = rows[j] * scale[j]
            for i in range(j + 1, 8):
                rows[i] = rows[i] - factor[i][j] * rows[j]
        done = rows[0]
        for i in range(1, 8):
            done = jnp.where(sublane == i, rows[i], done)
        panels[p] = done
        for q in range(p + 1, RANK // 8):
            column = [
                jnp.broadcast_to(panels[q][:, 8 * p + j : 8 * p + j + 1], full) for j in range(8)
            ]
            for j in range(8):
                column[j] = column[j] * scale[j]
                for i in range(j + 1, 8):
                    column[i] = column[i] - factor[i][j] * column[j]
            terms = [column[j] * rows[j] for j in range(8)]
            while len(terms) > 1:
                terms = [terms[n] + terms[n + 1] for n in range(0, len(terms), 2)]
            panels[q] = panels[q] - terms[0]
    return jnp.concatenate(panels, axis=0)[:, RANK:]


def refresh_kernel(
    dp_size,
    element_count,
    m_hbm,
    g_hbm,
    q_hbm,
    left_out,
    r_out,
    clip_out,
    m_ref,
    g_ref,
    q_ref,
    wide,
    other_m,
    other_g,
    sums,
    totals,
    tall,
    flat,
    own_far,
    own_near,
    far_in,
    far_out,
    near_in,
    near_out,
    tiles,
    w_high,
    w_mid,
    r_terms,
    z_terms,
    v_terms,
    v_ref,
    raw,
    lines,
    load,
    small_send,
    small_recv,
    big_send,
    big_recv,
    ring_send,
    far_recv,
    near_recv,
    gather_send,
    gather_far_recv,
    gather_near_recv,
    sib_send,
    sib_recv,
):
    me = lax.axis_index("etp")
    dp = lax.axis_index("dp")
    etp_size = 2 * RING
    chip = me // 2
    core = lax.rem(me, 2)
    sibling = chip * 2 + (1 - core)
    way = 1 - 2 * core
    ahead = lax.rem(chip + way + RING, RING) * 2 + core
    behind = lax.rem(chip - way + RING, RING) * 2 + core
    rows = m_ref.shape[0]

    loads = [
        pltpu.make_async_copy(source, target, load.at[n])
        for n, (source, target) in enumerate(((g_hbm, g_ref), (m_hbm, m_ref), (q_hbm, q_ref)))
    ]
    for copy in loads:
        copy.start()
    barrier = pltpu.get_barrier_semaphore()

    @pl.loop(1, etp_size)
    def _(step):
        pl.semaphore_signal(
            barrier, inc=1, device_id={"etp": lax.rem(me + step, etp_size)}, device_id_type=MESH
        )

    @pl.loop(1, dp_size)
    def _(step):
        pl.semaphore_signal(
            barrier, inc=1, device_id={"dp": lax.rem(dp + step, dp_size)}, device_id_type=MESH
        )

    loads[0].wait()
    wide[...] = g_ref[...].astype(F32)
    partial = jnp.zeros((8, BLOCK), F32)
    for b in range(BLOCKS):
        piece = wide[:, BLOCK * b : BLOCK * (b + 1)]
        partial = partial + jnp.sum((piece * piece).reshape(rows // 8, 8, BLOCK), axis=0)
    sums[me] = jnp.sum(partial, axis=0, keepdims=True)
    loads[1].wait()
    loads[2].wait()

    pl.semaphore_wait(barrier, etp_size + dp_size - 2)

    @pl.loop(1, etp_size)
    def _(step):
        pltpu.make_async_remote_copy(
            src_ref=sums.at[me],
            dst_ref=sums.at[me],
            send_sem=small_send.at[0],
            recv_sem=small_recv.at[0],
            device_id={"etp": lax.rem(me + step, etp_size)},
            device_id_type=MESH,
        ).start()

    copies = [
        pltpu.make_async_remote_copy(
            src_ref=source,
            dst_ref=target,
            send_sem=big_send.at[n],
            recv_sem=big_recv.at[n],
            device_id={"etp": sibling},
            device_id_type=MESH,
        )
        for n, (source, target) in enumerate(((m_ref, other_m), (wide, other_g)))
    ]
    for copy in copies:
        copy.start()

    others = sums.at[pl.ds(0, etp_size - 1)]
    pltpu.make_async_copy(others, others, small_recv.at[0]).wait()
    group = sums[0]
    for n in range(1, etp_size):
        group = group + sums[n]
    totals[dp] = group

    if dp_size > 1:

        @pl.loop(1, dp_size)
        def _(step):
            pltpu.make_async_remote_copy(
                src_ref=totals.at[dp],
                dst_ref=totals.at[dp],
                send_sem=small_send.at[1],
                recv_sem=small_recv.at[1],
                device_id={"dp": lax.rem(dp + step, dp_size)},
                device_id_type=MESH,
            ).start()

        far = totals.at[pl.ds(0, dp_size - 1)]
        pltpu.make_async_copy(far, far, small_recv.at[1]).wait()
        pltpu.make_async_copy(far, far, small_send.at[1]).wait()
    pltpu.make_async_copy(others, others, small_send.at[0]).wait()
    everything = totals[0]
    for n in range(1, dp_size):
        everything = everything + totals[n]
    total_sq = jnp.sum(everything, axis=1, keepdims=True)
    clip = jnp.minimum(1.0, lax.rsqrt(total_sq / element_count + epsilon))
    clip_out[...] = jnp.broadcast_to(clip, (8, BLOCK))
    for copy in copies:
        copy.wait()

    for b in range(BLOCKS):
        columns = slice(BLOCK * b, BLOCK * (b + 1))
        own = m_ref[:, columns] + clip * wide[:, columns]
        sib = other_m[:, columns] + clip * other_g[:, columns]
        blended = jnp.concatenate([own, sib], axis=0)
        for n, part in enumerate(split(blended, 2)):
            tall[b, :, BLOCK * n : BLOCK * (n + 1)] = part
            flat[b, BLOCK * n : BLOCK * (n + 1), :] = part.T

    def place(chunk, slot):
        tile = RING * slot + chunk
        row = lax.rem(tile, BLOCKS)
        return row, lax.rem(row + tile // BLOCKS + 1, BLOCKS)

    def is_pair(chunk, of_core):
        return of_core * ((chunk + 6) // RING)

    tile_row = lax.broadcasted_iota(jnp.int32, (BLOCK, BLOCK), 0)
    tile_column = lax.broadcasted_iota(jnp.int32, (BLOCK, BLOCK), 1)

    def product(row, column):
        both = nn(flat[row], tall[column])
        part = lambda i, j: both[BLOCK * i : BLOCK * (i + 1), BLOCK * j : BLOCK * (j + 1)]
        return part(0, 0) + (part(0, 1) + (part(1, 0) + part(1, 1)))

    def own_terms(store, chunk, s):
        if s is LAST:
            pair = is_pair(chunk, core)
            row, column = place(chunk, 3 + 5 * core)
            first = product(
                pair * (chunk - 2) + (1 - pair) * row, pair * (chunk - 2) + (1 - pair) * column
            )
            second = product(
                pair * (chunk + 4) + (1 - pair) * row, pair * (chunk + 4) + (1 - pair) * column
            )
            store[3 * BLOCK : 4 * BLOCK] = jnp.where(
                tile_row + (1 - pair) * BLOCK >= tile_column, first, second
            )
            diagonal = jnp.sum(
                jnp.where(tile_row == tile_column, second, 0.0), axis=0, keepdims=True
            )
            store[4 * BLOCK : 4 * BLOCK + 8] = jnp.broadcast_to(diagonal, (8, BLOCK))
        elif s is HALF:
            row, column = place(chunk, 4)
            start = pl.multiple_of(core * (BLOCK // 2), BLOCK // 2)
            rows_of = [flat[row, pl.ds(BLOCK * n + start, BLOCK // 2)] for n in range(2)]
            both = nn(jnp.concatenate(rows_of, axis=0), tall[column])
            upper, lower = both[: BLOCK // 2], both[BLOCK // 2 :]
            store[CHUNK - BLOCK // 2 :] = upper[:, :BLOCK] + (
                upper[:, BLOCK:] + (lower[:, :BLOCK] + lower[:, BLOCK:])
            )
        else:
            row, column = place(chunk, s + 5 * core)
            store[pl.ds(pl.multiple_of(BLOCK * s, BLOCK), BLOCK)] = product(row, column)

    def at(steps):
        return lax.rem(chip + way * steps + RING, RING)

    def index(s):
        return 3 if s is LAST else 4 if s is HALF else s

    def part_of(s):
        if s is LAST:
            return pl.ds(3 * BLOCK, SLOT)
        if s is HALF:
            return pl.ds(CHUNK - BLOCK // 2, BLOCK // 2)
        return pl.ds(pl.multiple_of(BLOCK * s, BLOCK), BLOCK)

    def slot_rows(slot, size=BLOCK):
        return pl.ds(pl.multiple_of(SLOT * slot, 8), size)

    def finished(chunk, of_core, s):
        if s is HALF:
            start = pl.multiple_of(4 * SLOT + of_core * (BLOCK // 2), 8)
            return tiles.at[chunk, pl.ds(start, BLOCK // 2)]
        return tiles.at[chunk, slot_rows(index(s) + 5 * of_core, SLOT if s is LAST else BLOCK)]

    def each(visit):
        @pl.loop(0, 3)
        def _(s):
            visit(s)

        visit(LAST)
        visit(HALF)

    def remote(source, target, send, recv, device):
        return pltpu.make_async_remote_copy(
            src_ref=source,
            dst_ref=target,
            send_sem=send,
            recv_sem=recv,
            device_id={"etp": device},
            device_id_type=MESH,
        )

    def far_copy(step, s):
        return remote(
            far_out.at[step, part_of(s)],
            far_in.at[step, part_of(s)],
            ring_send.at[0],
            far_recv.at[step, index(s)],
            ahead,
        )

    def near_copy(step, s):
        return remote(
            near_out.at[step, part_of(s)],
            near_in.at[step, part_of(s)],
            ring_send.at[1],
            near_recv.at[step, index(s)],
            behind,
        )

    def gather_far(step, chunk, s):
        view = finished(chunk, core, s)
        return remote(view, view, gather_send.at[0], gather_far_recv.at[step, index(s)], ahead)

    def gather_near(step, chunk, s):
        view = finished(chunk, core, s)
        return remote(view, view, gather_send.at[1], gather_near_recv.at[step, index(s)], behind)

    def sib_copy(order, chunk, of_core, s):
        view = finished(chunk, of_core, s)
        return remote(view, view, sib_send, sib_recv.at[order, index(s)], sibling)

    def store_tile(row, column, tile):
        for target, part in zip((w_high, w_mid), split(tile, 2)):
            target[row, column] = part

    def expand_slot(chunk, slot):
        row, column = place(chunk, slot)
        tile = tiles[chunk, slot_rows(slot)]
        store_tile(row, column, tile)
        store_tile(column, row, tile.T)

    def expand(chunk, of_core, s):
        if s is not LAST:
            expand_slot(chunk, s + 5 * of_core)
            return
        pair = is_pair(chunk, of_core)
        slot = 3 + 5 * of_core

        @pl.when(pair == 0)
        def _():
            expand_slot(chunk, slot)

        @pl.when(pair == 1)
        def _():
            tile = tiles[chunk, slot_rows(slot)]
            turned = tile.T
            start = pl.multiple_of(SLOT * slot + BLOCK, 8)
            diagonal = jnp.broadcast_to(tiles[chunk, pl.ds(start, 8)][0:1], (BLOCK, BLOCK))
            store_tile(chunk - 2, chunk - 2, jnp.where(tile_row >= tile_column, tile, turned))
            other = jnp.where(tile_row == tile_column, diagonal, turned)
            store_tile(
                chunk + 4, chunk + 4, jnp.where(tile_row < tile_column, tile, other)
            )

    def sib_expand(order, s):
        steps = 0 if order == 0 else (order + 1) // 2 if order % 2 else -(order // 2)
        sib_copy(order, at(steps), 1 - core, s).wait_recv()
        if s is HALF:
            expand_slot(at(steps), 4)
        else:
            expand(at(steps), 1 - core, s)

    def start_ring(s):
        own_terms(own_far, at(LONG), s)
        far_out[0, part_of(s)] = own_far[part_of(s)]
        far_copy(0, s).start()
        own_terms(own_near, at(-SHORT), s)
        near_out[0, part_of(s)] = own_near[part_of(s)]
        near_copy(0, s).start()

    def next_terms(s):
        own_terms(own_far, at(LONG - 1), s)
        own_terms(own_near, at(1 - SHORT), s)

    each(start_ring)
    each(next_terms)

    def pass_on(step, s):
        rows = part_of(s)
        far_copy(step - 1, s).wait_recv()
        far_out[step, rows] = own_far[rows] + far_in[step - 1, rows]
        far_copy(step, s).start()
        if step < SHORT:
            near_copy(step - 1, s).wait_recv()
            near_out[step, rows] = own_near[rows] + near_in[step - 1, rows]
            near_copy(step, s).start()
        own_terms(own_far, at(LONG - 1 - step), s)
        if step < SHORT - 1:
            own_terms(own_near, at(step + 1 - SHORT), s)

    for step in range(1, LONG):
        each(functools.partial(pass_on, step))

    def finish_sum(s):
        rows = part_of(s)
        near_copy(SHORT - 1, s).wait_recv()
        far_copy(LONG - 1, s).wait_recv()
        view = finished(chip, core, s)
        view[...] = own_far[rows] + near_in[SHORT - 1, rows] + far_in[LONG - 1, rows]
        gather_far(0, chip, s).start()
        gather_near(0, chip, s).start()
        sib_copy(0, chip, core, s).start()
        if s is not HALF:
            expand(chip, core, s)

    each(finish_sum)

    def spread(step, s):
        from_behind, from_ahead = at(-1 - step), at(1 + step)
        gather_far(step, from_behind, s).wait_recv()
        if step < LONG - 1:
            gather_far(step + 1, from_behind, s).start()
        sib_copy(2 * step + 1, from_behind, core, s).start()
        if step < SHORT:
            gather_near(step, from_ahead, s).wait_recv()
            if step < SHORT - 1:
                gather_near(step + 1, from_ahead, s).start()
            sib_copy(2 * step + 2, from_ahead, core, s).start()
        if s is not HALF:
            expand(from_behind, core, s)
            if step < SHORT:
                expand(from_ahead, core, s)
        for order in range(max(0, 2 * step - 1), 2 * step + 1):
            sib_expand(order, s)

    for step in range(LONG):
        each(functools.partial(spread, step))

    each(functools.partial(sib_expand, RING - 1))

    def keep(values, target):
        for n, part in enumerate(split(values, 3)):
            target[RANK * n : RANK * (n + 1), :] = part

    def gram_columns(terms, n):
        def weights(store):
            return jnp.concatenate(
                [
                    jnp.concatenate([store[i, 2 * n], store[i, 2 * n + 1]], axis=1)
                    for i in range(BLOCKS)
                ],
                axis=0,
            )

        first = nn(terms[...], weights(w_high))
        second = nn(terms[: 2 * RANK, :], weights(w_mid))
        v_ref[:, 2 * BLOCK * n : 2 * BLOCK * (n + 1)] = first[:RANK] + (
            (first[RANK : 2 * RANK] + second[:RANK]) + (first[2 * RANK :] + second[RANK:])
        )

    def small_gram():
        both = nt(r_terms[...], z_terms[...])
        part = lambda i, j: both[RANK * i : RANK * (i + 1), RANK * j : RANK * (j + 1)]
        return part(0, 0) + (
            (part(0, 1) + part(1, 0)) + (part(1, 1) + (part(0, 2) + part(2, 0)))
        )

    def apply(inverse, terms):
        high, middle, low = split(inverse, 3)
        none = jnp.zeros_like(high)
        stack = jnp.concatenate(
            [
                jnp.concatenate([high, high, high], axis=1),
                jnp.concatenate([middle, middle, none], axis=1),
                jnp.concatenate([low, none, none], axis=1),
            ],
            axis=0,
        )
        result = nn(stack, terms[...])
        return result[:RANK] + (result[RANK : 2 * RANK] + result[2 * RANK :])

    def normalise(across):
        return lax.rsqrt(jnp.sum(across * across, axis=1, keepdims=True) + epsilon)

    keep(q_ref[...], r_terms)

    @pl.loop(0, DIRECT)
    def _(turn):
        for n in range(BLOCKS // 2):
            gram_columns(r_terms, n)
        keep(v_ref[...], z_terms)
        inverse = inverse_cholesky(small_gram(), lines)
        across = apply(inverse, z_terms)
        keep(across * normalise(across), r_terms)

    for n in range(BLOCKS // 2):
        gram_columns(r_terms, n)
    keep(v_ref[...], z_terms)

    @pl.loop(DIRECT, ITERS - 1)
    def _(turn):
        inverse = inverse_cholesky(
            small_gram(),
            lines,
            [functools.partial(gram_columns, z_terms, n) for n in range(BLOCKS // 2)],
        )
        keep(v_ref[...], v_terms)
        across = apply(inverse, z_terms)
        ahead_of = apply(inverse, v_terms)
        scale = normalise(across)
        keep(across * scale, r_terms)
        keep(ahead_of * scale, z_terms)

    def last_raw():
        high, middle = (
            jnp.concatenate(
                [tall[b, :rows, BLOCK * n : BLOCK * (n + 1)] for b in range(BLOCKS)], axis=1
            )
            for n in range(2)
        )
        first = nt(high, r_terms[...])
        second = nt(middle, r_terms[: 2 * RANK, :])
        raw[...] = first[:, :RANK] + (
            (first[:, RANK : 2 * RANK] + second[:, :RANK])
            + (first[:, 2 * RANK :] + second[:, RANK:])
        )

    inverse = inverse_cholesky(small_gram(), lines, [last_raw])
    both = nt(
        jnp.concatenate(split(raw[...], 3), axis=0), jnp.concatenate(split(inverse, 3), axis=0)
    )
    part = lambda i, j: both[rows * i : rows * (i + 1), RANK * j : RANK * (j + 1)]
    left = part(0, 0) + ((part(0, 1) + part(1, 0)) + (part(1, 1) + (part(0, 2) + part(2, 0))))
    across = apply(inverse, z_terms)
    square = jnp.sum(across * across, axis=1, keepdims=True) + epsilon
    scale = lax.rsqrt(square)
    r_out[...] = across * scale
    same = lax.broadcasted_iota(jnp.int32, (RANK, RANK), 0) == lax.broadcasted_iota(
        jnp.int32, (RANK, RANK), 1
    )
    norm = jnp.sum(jnp.where(same, square * scale, 0.0), axis=0, keepdims=True)
    left_out[:, :RANK] = left * norm
    left_out[:, RANK:] = left

    for sent, semaphore in (
        (far_out, ring_send.at[0]),
        (near_out, ring_send.at[1]),
        (far_out, gather_send.at[0]),
        (near_out, gather_send.at[1]),
        (tiles.at[:, pl.ds(0, CHUNK)], sib_send),
    ):
        pltpu.make_async_copy(sent, sent, semaphore).wait()


def finish_kernel(m_ref, g_ref, clip_ref, left_ref, r_ref, m_out, q_out, u_out):
    blended = m_ref[...] + clip_ref[0:1, 0:1] * g_ref[...].astype(F32)
    rows = blended.shape[0]
    left = jnp.concatenate([left_ref[:, :RANK], left_ref[:, RANK:]], axis=0)
    high, middle = split(left, 2)
    right = split(r_ref[...], 2)
    outer = nn(
        jnp.concatenate([high, high, middle, middle], axis=1),
        jnp.concatenate(right + right, axis=0),
    )
    m_out[...] = blended - (1.0 - keep_rate) * outer[:rows]
    update_scale = math.sqrt(ROWS * COLS / RANK)
    u_out[...] = (update_scale * outer[rows:]).astype(BF16)
    q_out[...] = r_ref[...]


def body(momentum, grad, q_in):
    dp_size = lax.axis_size("dp")
    rows, cols = momentum.shape[1:]
    element_count = float(dp_size * rows * 2 * RING * cols)
    m, g, q = momentum[0], grad[0], q_in[0].T
    vmem = pl.BlockSpec(memory_space=pltpu.VMEM)
    hbm = pl.BlockSpec(memory_space=pl.ANY)
    tile = (BLOCK, BLOCK)
    dma = pltpu.SemaphoreType.DMA
    left, r_t, clip = pl.pallas_call(
        functools.partial(refresh_kernel, dp_size, element_count),
        out_shape=[
            pltpu.VMEM((rows, 2 * RANK), F32),
            pltpu.VMEM((RANK, cols), F32),
            pltpu.VMEM((8, BLOCK), F32),
        ],
        in_specs=[hbm] * 3,
        out_specs=[vmem] * 3,
        scratch_shapes=[
            pltpu.VMEM((rows, cols), F32),
            pltpu.VMEM((rows, cols), BF16),
            pltpu.VMEM((RANK, cols), F32),
            pltpu.VMEM((rows, cols), F32),
            pltpu.VMEM((rows, cols), F32),
            pltpu.VMEM((rows, cols), F32),
            pltpu.VMEM((2 * RING, 1, BLOCK), F32),
            pltpu.VMEM((dp_size, 1, BLOCK), F32),
            pltpu.VMEM((BLOCKS, 2 * rows, 2 * BLOCK), BF16),
            pltpu.VMEM((BLOCKS, 2 * BLOCK, 2 * rows), BF16),
            pltpu.VMEM((CHUNK, BLOCK), F32),
            pltpu.VMEM((CHUNK, BLOCK), F32),
            pltpu.VMEM((LONG, CHUNK, BLOCK), F32),
            pltpu.VMEM((LONG, CHUNK, BLOCK), F32),
            pltpu.VMEM((SHORT, CHUNK, BLOCK), F32),
            pltpu.VMEM((SHORT, CHUNK, BLOCK), F32),
            pltpu.VMEM((RING, SLOTS * SLOT, BLOCK), F32),
            pltpu.VMEM((BLOCKS, BLOCKS) + tile, BF16),
            pltpu.VMEM((BLOCKS, BLOCKS) + tile, BF16),
            pltpu.VMEM((3 * RANK, cols), BF16),
            pltpu.VMEM((3 * RANK, cols), BF16),
            pltpu.VMEM((3 * RANK, cols), BF16),
            pltpu.VMEM((RANK, cols), F32),
            pltpu.VMEM((rows, RANK), F32),
            pltpu.VMEM((RANK // 8 + RANK, 8, 2 * RANK), F32),
            dma((3,)),
            dma((2,)),
            dma((2,)),
            dma((2,)),
            dma((2,)),
            dma((2,)),
            dma((LONG, 5)),
            dma((SHORT, 5)),
            dma((2,)),
            dma((LONG, 5)),
            dma((SHORT, 5)),
            dma,
            dma((RING, 5)),
        ],
        compiler_params=pltpu.CompilerParams(
            collective_id=0, has_side_effects=True, vmem_limit_bytes=56 << 20
        ),
    )(m, g, q)
    part = rows // 2
    whole = lambda shape: pl.BlockSpec(shape, lambda n: (0, 0))
    by_rows = pl.BlockSpec((part, cols), lambda n: (n, 0))
    m_new, q_new, update = pl.pallas_call(
        finish_kernel,
        grid=(2,),
        out_shape=[
            jax.ShapeDtypeStruct((rows, cols), F32),
            jax.ShapeDtypeStruct((RANK, cols), F32),
            jax.ShapeDtypeStruct((rows, cols), BF16),
        ],
        in_specs=[
            by_rows,
            by_rows,
            whole((8, BLOCK)),
            pl.BlockSpec((part, 2 * RANK), lambda n: (n, 0)),
            whole((RANK, cols)),
        ],
        out_specs=[by_rows, whole((RANK, cols)), by_rows],
        compiler_params=pltpu.CompilerParams(vmem_limit_bytes=24 << 20),
    )(m, g, clip, left, r_t)
    return m_new[None], q_new.T[None], update[None]


def solution(mesh):
    return jax.shard_map(
        body,
        mesh=mesh,
        in_specs=(P("dp", "etp", None), P("dp", "etp", None), P("dp", None, None)),
        out_specs=(P("dp", "etp", None), P("dp", None, None), P("dp", "etp", None)),
        check_vma=False,
    )
```

```python
import functools
import math

import jax
import jax.numpy as jnp
from jax import lax
from jax.experimental import pallas as pl
from jax.experimental.pallas import tpu as pltpu
from jax.sharding import PartitionSpec as P

ROWS = 3584
COLS = 1536
RANK = 64
ITERS = 8
DIRECT = 3

BLOCK = 128
BLOCKS = COLS // BLOCK
SLOTS = 9
SLOT = BLOCK + 8
CHUNK = 4 * BLOCK + 8 + BLOCK // 2
RING = 8
LONG = RING // 2
SHORT = RING - 1 - LONG

LAST, HALF = "last", "half"

keep_rate = 0.9
epsilon = 1e-06

MESH = pl.DeviceIdType.MESH
F32 = jnp.float32
BF16 = jnp.bfloat16


def nn(former, latter):
    return jnp.dot(former, latter, preferred_element_type=F32)


def nt(former, latter):
    return lax.dot_general(former, latter, (((1,), (1,)), ((), ())), preferred_element_type=F32)


def split(values, terms):
    parts = []
    for _ in range(terms):
        parts.append(values.astype(BF16))
        values = values - parts[-1].astype(F32)
    return parts


def inverse_cholesky(gram, lines, between=()):
    full = (8, 2 * RANK)
    ones = lax.broadcasted_iota(jnp.int32, (RANK, RANK), 0) == lax.broadcasted_iota(
        jnp.int32, (RANK, RANK), 1
    )
    joined = jnp.concatenate([gram, ones.astype(F32)], axis=1)
    panels = [joined[8 * p : 8 * p + 8] for p in range(RANK // 8)]
    sublane = lax.broadcasted_iota(jnp.int32, full, 0)

    def across_lanes(values, first):
        return [
            jnp.broadcast_to(values[:, first + j : first + j + 1], full) for j in range(8)
        ]

    def line(at, values, i):
        if i == 0:
            lines[at] = values
        return jnp.broadcast_to(lines[at, i : i + 1, :], full)

    diagonal = across_lanes(panels[0], 0)
    for p in range(RANK // 8):
        if p < len(between):
            between[p]()
        start = 17 * p
        rows = [line(start, panels[p], i) for i in range(8)]
        entry = [[None] * 8 for _ in range(8)]
        for j in range(8):
            for i in range(8):
                entry[i][j] = line(start + 1 + j, diagonal[j], i)
        ahead = p + 1 < RANK // 8
        if ahead:
            beside = across_lanes(panels[p + 1], 8 * p)
            diagonal = across_lanes(panels[p + 1], 8 * p + 8)
        scale = [None] * 8
        factor = [[None] * 8 for _ in range(8)]
        for j in range(8):
            scale[j] = lax.rsqrt(entry[j][j])
            for i in range(j + 1, 8):
                factor[i][j] = entry[i][j] * scale[j]
            for i in range(j + 1, 8):
                for m in range(j + 1, i + 1):
                    entry[i][m] = entry[i][m] - factor[i][j] * factor[m][j]
            if ahead:
                beside[j] = beside[j] * scale[j]
                for i in range(j + 1, 8):
                    beside[i] = beside[i] - factor[i][j] * beside[j]
                for i in range(8):
                    diagonal[i] = diagonal[i] - beside[j] * line(start + 9 + j, beside[j], i)
            rows[j] = rows[j] * scale[j]
            for i in range(j + 1, 8):
                rows[i] = rows[i] - factor[i][j] * rows[j]
        done = rows[0]
        for i in range(1, 8):
            done = jnp.where(sublane == i, rows[i], done)
        panels[p] = done
        for q in range(p + 1, RANK // 8):
            columns = beside
            if q > p + 1:
                columns = across_lanes(panels[q], 8 * p)
                for j in range(8):
                    columns[j] = columns[j] * scale[j]
                    for i in range(j + 1, 8):
                        columns[i] = columns[i] - factor[i][j] * columns[j]
            terms = [columns[j] * rows[j] for j in range(8)]
            while len(terms) > 1:
                terms = [terms[n] + terms[n + 1] for n in range(0, len(terms), 2)]
            panels[q] = panels[q] - terms[0]
    return jnp.concatenate(panels, axis=0)[:, RANK:]


def refresh_kernel(
    dp_size,
    element_count,
    m_hbm,
    g_hbm,
    q_hbm,
    left_out,
    r_out,
    clip_out,
    m_ref,
    g_ref,
    q_ref,
    wide,
    other_m,
    other_g,
    sums,
    totals,
    tall,
    flat,
    own_far,
    own_near,
    far_in,
    far_out,
    near_in,
    near_out,
    tiles,
    w_high,
    w_mid,
    r_terms,
    z_terms,
    v_terms,
    v_ref,
    raw,
    lines,
    load,
    small_send,
    small_recv,
    big_send,
    big_recv,
    ring_send,
    far_recv,
    near_recv,
    gather_send,
    gather_far_recv,
    gather_near_recv,
    sib_send,
    sib_recv,
):
    me = lax.axis_index("etp")
    dp = lax.axis_index("dp")
    etp_size = 2 * RING
    chip = me // 2
    core = lax.rem(me, 2)
    sibling = chip * 2 + (1 - core)
    way = 1 - 2 * core
    ahead = lax.rem(chip + way + RING, RING) * 2 + core
    behind = lax.rem(chip - way + RING, RING) * 2 + core
    rows = m_ref.shape[0]

    loads = [
        pltpu.make_async_copy(source, target, load.at[n])
        for n, (source, target) in enumerate(((g_hbm, g_ref), (m_hbm, m_ref), (q_hbm, q_ref)))
    ]
    for copy in loads:
        copy.start()
    barrier = pltpu.get_barrier_semaphore()

    @pl.loop(1, etp_size)
    def _(step):
        pl.semaphore_signal(
            barrier, inc=1, device_id={"etp": lax.rem(me + step, etp_size)}, device_id_type=MESH
        )

    @pl.loop(1, dp_size)
    def _(step):
        pl.semaphore_signal(
            barrier, inc=1, device_id={"dp": lax.rem(dp + step, dp_size)}, device_id_type=MESH
        )

    loads[0].wait()
    wide[...] = g_ref[...].astype(F32)
    partial = jnp.zeros((8, BLOCK), F32)
    for b in range(BLOCKS):
        piece = wide[:, BLOCK * b : BLOCK * (b + 1)]
        partial = partial + jnp.sum((piece * piece).reshape(rows // 8, 8, BLOCK), axis=0)
    sums[me] = jnp.sum(partial, axis=0, keepdims=True)
    loads[1].wait()
    loads[2].wait()

    pl.semaphore_wait(barrier, etp_size + dp_size - 2)

    @pl.loop(1, etp_size)
    def _(step):
        pltpu.make_async_remote_copy(
            src_ref=sums.at[me],
            dst_ref=sums.at[me],
            send_sem=small_send.at[0],
            recv_sem=small_recv.at[0],
            device_id={"etp": lax.rem(me + step, etp_size)},
            device_id_type=MESH,
        ).start()

    copies = [
        pltpu.make_async_remote_copy(
            src_ref=source,
            dst_ref=target,
            send_sem=big_send.at[n],
            recv_sem=big_recv.at[n],
            device_id={"etp": sibling},
            device_id_type=MESH,
        )
        for n, (source, target) in enumerate(((m_ref, other_m), (wide, other_g)))
    ]
    for copy in copies:
        copy.start()

    others = sums.at[pl.ds(0, etp_size - 1)]
    pltpu.make_async_copy(others, others, small_recv.at[0]).wait()
    group = sums[0]
    for n in range(1, etp_size):
        group = group + sums[n]
    totals[dp] = group

    if dp_size > 1:

        @pl.loop(1, dp_size)
        def _(step):
            pltpu.make_async_remote_copy(
                src_ref=totals.at[dp],
                dst_ref=totals.at[dp],
                send_sem=small_send.at[1],
                recv_sem=small_recv.at[1],
                device_id={"dp": lax.rem(dp + step, dp_size)},
                device_id_type=MESH,
            ).start()

        far = totals.at[pl.ds(0, dp_size - 1)]
        pltpu.make_async_copy(far, far, small_recv.at[1]).wait()
        pltpu.make_async_copy(far, far, small_send.at[1]).wait()
    pltpu.make_async_copy(others, others, small_send.at[0]).wait()
    everything = totals[0]
    for n in range(1, dp_size):
        everything = everything + totals[n]
    total_sq = jnp.sum(everything, axis=1, keepdims=True)
    clip = jnp.minimum(1.0, lax.rsqrt(total_sq / element_count + epsilon))
    clip_out[...] = jnp.broadcast_to(clip, (8, BLOCK))
    for copy in copies:
        copy.wait()

    for b in range(BLOCKS):
        columns = slice(BLOCK * b, BLOCK * (b + 1))
        own = m_ref[:, columns] + clip * wide[:, columns]
        sib = other_m[:, columns] + clip * other_g[:, columns]
        blended = jnp.concatenate([own, sib], axis=0)
        for n, part in enumerate(split(blended, 2)):
            tall[b, :, BLOCK * n : BLOCK * (n + 1)] = part
            flat[b, BLOCK * n : BLOCK * (n + 1), :] = part.T

    def place(chunk, slot):
        tile = RING * slot + chunk
        row = lax.rem(tile, BLOCKS)
        return row, lax.rem(row + tile // BLOCKS + 1, BLOCKS)

    def is_pair(chunk, of_core):
        return of_core * ((chunk + 6) // RING)

    tile_row = lax.broadcasted_iota(jnp.int32, (BLOCK, BLOCK), 0)
    tile_column = lax.broadcasted_iota(jnp.int32, (BLOCK, BLOCK), 1)

    def product(row, column):
        both = nn(flat[row], tall[column])
        part = lambda i, j: both[BLOCK * i : BLOCK * (i + 1), BLOCK * j : BLOCK * (j + 1)]
        return part(0, 0) + (part(0, 1) + (part(1, 0) + part(1, 1)))

    def own_terms(store, chunk, s):
        if s is LAST:
            pair = is_pair(chunk, core)
            row, column = place(chunk, 3 + 5 * core)
            first = product(
                pair * (chunk - 2) + (1 - pair) * row, pair * (chunk - 2) + (1 - pair) * column
            )
            second = product(
                pair * (chunk + 4) + (1 - pair) * row, pair * (chunk + 4) + (1 - pair) * column
            )
            store[3 * BLOCK : 4 * BLOCK] = jnp.where(
                tile_row + (1 - pair) * BLOCK >= tile_column, first, second
            )
            diagonal = jnp.sum(
                jnp.where(tile_row == tile_column, second, 0.0), axis=0, keepdims=True
            )
            store[4 * BLOCK : 4 * BLOCK + 8] = jnp.broadcast_to(diagonal, (8, BLOCK))
        elif s is HALF:
            row, column = place(chunk, 4)
            start = pl.multiple_of(core * (BLOCK // 2), BLOCK // 2)
            rows_of = [flat[row, pl.ds(BLOCK * n + start, BLOCK // 2)] for n in range(2)]
            both = nn(jnp.concatenate(rows_of, axis=0), tall[column])
            upper, lower = both[: BLOCK // 2], both[BLOCK // 2 :]
            store[CHUNK - BLOCK // 2 :] = upper[:, :BLOCK] + (
                upper[:, BLOCK:] + (lower[:, :BLOCK] + lower[:, BLOCK:])
            )
        else:
            row, column = place(chunk, s + 5 * core)
            store[pl.ds(pl.multiple_of(BLOCK * s, BLOCK), BLOCK)] = product(row, column)

    def at(steps):
        return lax.rem(chip + way * steps + RING, RING)

    def index(s):
        return 3 if s is LAST else 4 if s is HALF else s

    def part_of(s):
        if s is LAST:
            return pl.ds(3 * BLOCK, SLOT)
        if s is HALF:
            return pl.ds(CHUNK - BLOCK // 2, BLOCK // 2)
        return pl.ds(pl.multiple_of(BLOCK * s, BLOCK), BLOCK)

    def slot_rows(slot, size=BLOCK):
        return pl.ds(pl.multiple_of(SLOT * slot, 8), size)

    def finished(chunk, of_core, s):
        if s is HALF:
            start = pl.multiple_of(4 * SLOT + of_core * (BLOCK // 2), 8)
            return tiles.at[chunk, pl.ds(start, BLOCK // 2)]
        return tiles.at[chunk, slot_rows(index(s) + 5 * of_core, SLOT if s is LAST else BLOCK)]

    def each(visit):
        @pl.loop(0, 3)
        def _(s):
            visit(s)

        visit(LAST)
        visit(HALF)

    def remote(source, target, send, recv, device):
        return pltpu.make_async_remote_copy(
            src_ref=source,
            dst_ref=target,
            send_sem=send,
            recv_sem=recv,
            device_id={"etp": device},
            device_id_type=MESH,
        )

    def far_copy(step, s):
        return remote(
            far_out.at[step, part_of(s)],
            far_in.at[step, part_of(s)],
            ring_send.at[0],
            far_recv.at[step, index(s)],
            ahead,
        )

    def near_copy(step, s):
        return remote(
            near_out.at[step, part_of(s)],
            near_in.at[step, part_of(s)],
            ring_send.at[1],
            near_recv.at[step, index(s)],
            behind,
        )

    def gather_far(step, chunk, s):
        view = finished(chunk, core, s)
        return remote(view, view, gather_send.at[0], gather_far_recv.at[step, index(s)], ahead)

    def gather_near(step, chunk, s):
        view = finished(chunk, core, s)
        return remote(view, view, gather_send.at[1], gather_near_recv.at[step, index(s)], behind)

    def sib_copy(order, chunk, of_core, s):
        view = finished(chunk, of_core, s)
        return remote(view, view, sib_send, sib_recv.at[order, index(s)], sibling)

    def store_tile(row, column, tile):
        for target, part in zip((w_high, w_mid), split(tile, 2)):
            target[row, column] = part

    def expand_slot(chunk, slot):
        row, column = place(chunk, slot)
        tile = tiles[chunk, slot_rows(slot)]
        store_tile(row, column, tile)
        store_tile(column, row, tile.T)

    def expand(chunk, of_core, s):
        if s is not LAST:
            expand_slot(chunk, s + 5 * of_core)
            return
        pair = is_pair(chunk, of_core)
        slot = 3 + 5 * of_core

        @pl.when(pair == 0)
        def _():
            expand_slot(chunk, slot)

        @pl.when(pair == 1)
        def _():
            tile = tiles[chunk, slot_rows(slot)]
            turned = tile.T
            start = pl.multiple_of(SLOT * slot + BLOCK, 8)
            diagonal = jnp.broadcast_to(tiles[chunk, pl.ds(start, 8)][0:1], (BLOCK, BLOCK))
            store_tile(chunk - 2, chunk - 2, jnp.where(tile_row >= tile_column, tile, turned))
            other = jnp.where(tile_row == tile_column, diagonal, turned)
            store_tile(
                chunk + 4, chunk + 4, jnp.where(tile_row < tile_column, tile, other)
            )

    def sib_expand(order, s):
        steps = 0 if order == 0 else (order + 1) // 2 if order % 2 else -(order // 2)
        sib_copy(order, at(steps), 1 - core, s).wait_recv()
        if s is HALF:
            expand_slot(at(steps), 4)
        else:
            expand(at(steps), 1 - core, s)

    def start_ring(s):
        own_terms(own_far, at(LONG), s)
        far_out[0, part_of(s)] = own_far[part_of(s)]
        far_copy(0, s).start()
        own_terms(own_near, at(-SHORT), s)
        near_out[0, part_of(s)] = own_near[part_of(s)]
        near_copy(0, s).start()

    def next_terms(s):
        own_terms(own_far, at(LONG - 1), s)
        own_terms(own_near, at(1 - SHORT), s)

    each(start_ring)
    each(next_terms)

    def pass_on(step, s):
        rows = part_of(s)
        far_copy(step - 1, s).wait_recv()
        far_out[step, rows] = own_far[rows] + far_in[step - 1, rows]
        far_copy(step, s).start()
        if step < SHORT:
            near_copy(step - 1, s).wait_recv()
            near_out[step, rows] = own_near[rows] + near_in[step - 1, rows]
            near_copy(step, s).start()
        own_terms(own_far, at(LONG - 1 - step), s)
        if step < SHORT - 1:
            own_terms(own_near, at(step + 1 - SHORT), s)

    for step in range(1, LONG):
        each(functools.partial(pass_on, step))

    def finish_sum(s):
        rows = part_of(s)
        near_copy(SHORT - 1, s).wait_recv()
        far_copy(LONG - 1, s).wait_recv()
        view = finished(chip, core, s)
        view[...] = own_far[rows] + near_in[SHORT - 1, rows] + far_in[LONG - 1, rows]
        gather_far(0, chip, s).start()
        gather_near(0, chip, s).start()
        sib_copy(0, chip, core, s).start()
        if s is not HALF:
            expand(chip, core, s)

    each(finish_sum)

    def spread(step, s):
        from_behind, from_ahead = at(-1 - step), at(1 + step)
        gather_far(step, from_behind, s).wait_recv()
        if step < LONG - 1:
            gather_far(step + 1, from_behind, s).start()
        sib_copy(2 * step + 1, from_behind, core, s).start()
        if step < SHORT:
            gather_near(step, from_ahead, s).wait_recv()
            if step < SHORT - 1:
                gather_near(step + 1, from_ahead, s).start()
            sib_copy(2 * step + 2, from_ahead, core, s).start()
        if s is not HALF:
            expand(from_behind, core, s)
            if step < SHORT:
                expand(from_ahead, core, s)
        for order in range(max(0, 2 * step - 1), 2 * step + 1):
            sib_expand(order, s)

    for step in range(LONG):
        each(functools.partial(spread, step))

    each(functools.partial(sib_expand, RING - 1))

    def keep(values, target):
        for n, part in enumerate(split(values, 3)):
            target[RANK * n : RANK * (n + 1), :] = part

    def gram_columns(terms, n):
        def weights(store):
            return jnp.concatenate(
                [
                    jnp.concatenate([store[i, 2 * n], store[i, 2 * n + 1]], axis=1)
                    for i in range(BLOCKS)
                ],
                axis=0,
            )

        first = nn(terms[...], weights(w_high))
        second = nn(terms[: 2 * RANK, :], weights(w_mid))
        v_ref[:, 2 * BLOCK * n : 2 * BLOCK * (n + 1)] = first[:RANK] + (
            (first[RANK : 2 * RANK] + second[:RANK]) + (first[2 * RANK :] + second[RANK:])
        )

    def small_gram():
        both = nt(r_terms[...], z_terms[...])
        part = lambda i, j: both[RANK * i : RANK * (i + 1), RANK * j : RANK * (j + 1)]
        return part(0, 0) + (
            (part(0, 1) + part(1, 0)) + (part(1, 1) + (part(0, 2) + part(2, 0)))
        )

    def apply(inverse, terms):
        high, middle, low = split(inverse, 3)
        none = jnp.zeros_like(high)
        stack = jnp.concatenate(
            [
                jnp.concatenate([high, high, high], axis=1),
                jnp.concatenate([middle, middle, none], axis=1),
                jnp.concatenate([low, none, none], axis=1),
            ],
            axis=0,
        )
        result = nn(stack, terms[...])
        return result[:RANK] + (result[RANK : 2 * RANK] + result[2 * RANK :])

    def normalise(across):
        return lax.rsqrt(jnp.sum(across * across, axis=1, keepdims=True) + epsilon)

    keep(q_ref[...], r_terms)

    @pl.loop(0, DIRECT)
    def _(turn):
        for n in range(BLOCKS // 2):
            gram_columns(r_terms, n)
        keep(v_ref[...], z_terms)
        inverse = inverse_cholesky(small_gram(), lines)
        across = apply(inverse, z_terms)
        keep(across * normalise(across), r_terms)

    for n in range(BLOCKS // 2):
        gram_columns(r_terms, n)
    keep(v_ref[...], z_terms)

    @pl.loop(DIRECT, ITERS - 1)
    def _(turn):
        inverse = inverse_cholesky(
            small_gram(),
            lines,
            [functools.partial(gram_columns, z_terms, n) for n in range(BLOCKS // 2)],
        )
        keep(v_ref[...], v_terms)
        across = apply(inverse, z_terms)
        ahead_of = apply(inverse, v_terms)
        scale = normalise(across)
        keep(across * scale, r_terms)
        keep(ahead_of * scale, z_terms)

    def last_raw():
        high, middle = (
            jnp.concatenate(
                [tall[b, :rows, BLOCK * n : BLOCK * (n + 1)] for b in range(BLOCKS)], axis=1
            )
            for n in range(2)
        )
        first = nt(high, r_terms[...])
        second = nt(middle, r_terms[: 2 * RANK, :])
        raw[...] = first[:, :RANK] + (
            (first[:, RANK : 2 * RANK] + second[:, :RANK])
            + (first[:, 2 * RANK :] + second[:, RANK:])
        )

    inverse = inverse_cholesky(small_gram(), lines, [last_raw])
    both = nt(
        jnp.concatenate(split(raw[...], 3), axis=0), jnp.concatenate(split(inverse, 3), axis=0)
    )
    part = lambda i, j: both[rows * i : rows * (i + 1), RANK * j : RANK * (j + 1)]
    left = part(0, 0) + ((part(0, 1) + part(1, 0)) + (part(1, 1) + (part(0, 2) + part(2, 0))))
    across = apply(inverse, z_terms)
    square = jnp.sum(across * across, axis=1, keepdims=True) + epsilon
    scale = lax.rsqrt(square)
    r_out[...] = across * scale
    same = lax.broadcasted_iota(jnp.int32, (RANK, RANK), 0) == lax.broadcasted_iota(
        jnp.int32, (RANK, RANK), 1
    )
    norm = jnp.sum(jnp.where(same, square * scale, 0.0), axis=0, keepdims=True)
    left_out[:, :RANK] = left * norm
    left_out[:, RANK:] = left

    for sent, semaphore in (
        (far_out, ring_send.at[0]),
        (near_out, ring_send.at[1]),
        (far_out, gather_send.at[0]),
        (near_out, gather_send.at[1]),
        (tiles.at[:, pl.ds(0, CHUNK)], sib_send),
    ):
        pltpu.make_async_copy(sent, sent, semaphore).wait()


def finish_kernel(m_ref, g_ref, clip_ref, left_ref, r_ref, m_out, q_out, u_out):
    blended = m_ref[...] + clip_ref[0:1, 0:1] * g_ref[...].astype(F32)
    rows = blended.shape[0]
    left = jnp.concatenate([left_ref[:, :RANK], left_ref[:, RANK:]], axis=0)
    high, middle = split(left, 2)
    right = split(r_ref[...], 2)
    outer = nn(
        jnp.concatenate([high, high, middle, middle], axis=1),
        jnp.concatenate(right + right, axis=0),
    )
    m_out[...] = blended - (1.0 - keep_rate) * outer[:rows]
    update_scale = math.sqrt(ROWS * COLS / RANK)
    u_out[...] = (update_scale * outer[rows:]).astype(BF16)
    q_out[...] = r_ref[...]


def body(momentum, grad, q_in):
    dp_size = lax.axis_size("dp")
    rows, cols = momentum.shape[1:]
    element_count = float(dp_size * rows * 2 * RING * cols)
    m, g, q = momentum[0], grad[0], q_in[0].T
    vmem = pl.BlockSpec(memory_space=pltpu.VMEM)
    hbm = pl.BlockSpec(memory_space=pl.ANY)
    tile = (BLOCK, BLOCK)
    dma = pltpu.SemaphoreType.DMA
    left, r_t, clip = pl.pallas_call(
        functools.partial(refresh_kernel, dp_size, element_count),
        out_shape=[
            pltpu.VMEM((rows, 2 * RANK), F32),
            pltpu.VMEM((RANK, cols), F32),
            pltpu.VMEM((8, BLOCK), F32),
        ],
        in_specs=[hbm] * 3,
        out_specs=[vmem] * 3,
        scratch_shapes=[
            pltpu.VMEM((rows, cols), F32),
            pltpu.VMEM((rows, cols), BF16),
            pltpu.VMEM((RANK, cols), F32),
            pltpu.VMEM((rows, cols), F32),
            pltpu.VMEM((rows, cols), F32),
            pltpu.VMEM((rows, cols), F32),
            pltpu.VMEM((2 * RING, 1, BLOCK), F32),
            pltpu.VMEM((dp_size, 1, BLOCK), F32),
            pltpu.VMEM((BLOCKS, 2 * rows, 2 * BLOCK), BF16),
            pltpu.VMEM((BLOCKS, 2 * BLOCK, 2 * rows), BF16),
            pltpu.VMEM((CHUNK, BLOCK), F32),
            pltpu.VMEM((CHUNK, BLOCK), F32),
            pltpu.VMEM((LONG, CHUNK, BLOCK), F32),
            pltpu.VMEM((LONG, CHUNK, BLOCK), F32),
            pltpu.VMEM((SHORT, CHUNK, BLOCK), F32),
            pltpu.VMEM((SHORT, CHUNK, BLOCK), F32),
            pltpu.VMEM((RING, SLOTS * SLOT, BLOCK), F32),
            pltpu.VMEM((BLOCKS, BLOCKS) + tile, BF16),
            pltpu.VMEM((BLOCKS, BLOCKS) + tile, BF16),
            pltpu.VMEM((3 * RANK, cols), BF16),
            pltpu.VMEM((3 * RANK, cols), BF16),
            pltpu.VMEM((3 * RANK, cols), BF16),
            pltpu.VMEM((RANK, cols), F32),
            pltpu.VMEM((rows, RANK), F32),
            pltpu.VMEM((17 * RANK // 8, 8, 2 * RANK), F32),
            dma((3,)),
            dma((2,)),
            dma((2,)),
            dma((2,)),
            dma((2,)),
            dma((2,)),
            dma((LONG, 5)),
            dma((SHORT, 5)),
            dma((2,)),
            dma((LONG, 5)),
            dma((SHORT, 5)),
            dma,
            dma((RING, 5)),
        ],
        compiler_params=pltpu.CompilerParams(
            collective_id=0, has_side_effects=True, vmem_limit_bytes=56 << 20
        ),
    )(m, g, q)
    part = rows // 2
    whole = lambda shape: pl.BlockSpec(shape, lambda n: (0, 0))
    by_rows = pl.BlockSpec((part, cols), lambda n: (n, 0))
    m_new, q_new, update = pl.pallas_call(
        finish_kernel,
        grid=(2,),
        out_shape=[
            jax.ShapeDtypeStruct((rows, cols), F32),
            jax.ShapeDtypeStruct((RANK, cols), F32),
            jax.ShapeDtypeStruct((rows, cols), BF16),
        ],
        in_specs=[
            by_rows,
            by_rows,
            whole((8, BLOCK)),
            pl.BlockSpec((part, 2 * RANK), lambda n: (n, 0)),
            whole((RANK, cols)),
        ],
        out_specs=[by_rows, whole((RANK, cols)), by_rows],
        compiler_params=pltpu.CompilerParams(vmem_limit_bytes=24 << 20),
    )(m, g, clip, left, r_t)
    return m_new[None], q_new.T[None], update[None]


def solution(mesh):
    return jax.shard_map(
        body,
        mesh=mesh,
        in_specs=(P("dp", "etp", None), P("dp", "etp", None), P("dp", None, None)),
        out_specs=(P("dp", "etp", None), P("dp", None, None), P("dp", "etp", None)),
        check_vma=False,
    )
```
